32 devices in a mesh: dp: 16 (over z, y, x), tensor: 2 (over core).
Axes of the slice: x: 2, y: 2, z: 4, core: 2. Of those that a mesh axis runs over, the one named last changes fastest.
Arguments:
- inputs: bfloat16 [2, 8192, 1024], P(None, ('dp', 'tensor')), may hold values from -6 to 6
- lengths: int32 [2, 16, 8], P(None, 'dp'), may hold values from 0 to 512, as said below
- query_weight: bfloat16 [1024, 1024], P(None, 'tensor'), may hold values from -0.1875 to 0.1875
- key_weight: bfloat16 [1024, 1024], P(None, 'tensor'), may hold values from -0.1875 to 0.1875
- value_weight: bfloat16 [1024, 1024], P(None, 'tensor'), may hold values from -0.1875 to 0.1875
- output_weight: bfloat16 [1024, 1024], P('tensor'), may hold values from -0.1875 to 0.1875
- inner_weight: bfloat16 [1024, 4096], P(None, 'tensor'), may hold values from -0.1875 to 0.1875
- outer_weight: bfloat16 [4096, 1024], P('tensor'), may hold values from -0.09375 to 0.09375
- entry_gain: float32 [1024], replicated, may hold values from 0.25 to 1.75
- entry_bias: float32 [1024], replicated, may hold values from -3 to 3
- merge_gain: float32 [1024], replicated, may hold values from 0.25 to 1.75
- merge_bias: float32 [1024], replicated, may hold values from -3 to 3
- inlet_gain: float32 [1024], replicated, may hold values from 0.25 to 1.75
- inlet_bias: float32 [1024], replicated, may hold values from -3 to 3
- outlet_gain: float32 [1024], replicated, may hold values from 0.25 to 1.75
- outlet_bias: float32 [1024], replicated, may hold values from -3 to 3
- cotangent: bfloat16 [2, 8192, 1024], P(None, ('dp', 'tensor')), may hold values from -6 to 6
Outputs:
- outputs: bfloat16 [2, 8192, 1024], P(None, ('dp', 'tensor'))
- input_grad: bfloat16 [2, 8192, 1024], P(None, ('dp', 'tensor'))
- query_grad: float32 [1024, 1024], P(None, 'tensor')
- key_grad: float32 [1024, 1024], P(None, 'tensor')
- value_grad: float32 [1024, 1024], P(None, 'tensor')
- output_grad: float32 [1024, 1024], P('tensor')
- inner_grad: float32 [1024, 4096], P(None, 'tensor')
- outer_grad: float32 [4096, 1024], P('tensor')
- gain_entry: float32 [1024], replicated
- bias_entry: float32 [1024], replicated
- gain_merge: float32 [1024], replicated
- bias_merge: float32 [1024], replicated
- gain_inlet: float32 [1024], replicated
- bias_inlet: float32 [1024], replicated
- gain_outlet: float32 [1024], replicated
- bias_outlet: float32 [1024], replicated
The draws below stay inside these ranges and needn't reach their ends.
Inputs may be any that keep to these rules, and one draw needn't show every extreme that they name: `lengths`: each row lists the 8 sequences of one buffer packed in order from its first row; they sum to at most 512, the rest of the buffer is padding; slots may be empty; some buffer holds a single sequence of exactly 512.
All inputs are finite; a program needn't handle non-finite values.
Results may differ from the reference program's by a relative error of at most 0.015.
The reference program's roundings to bfloat16 on the way count: a program that leaves them out, or rounds other values in their place, can miss the bound.
Values may be sent and summed in bfloat16 or wider, within the bound.
No kernel may reach another device: no remote copies, remote signals or barrier semaphores. Data moves between devices by JAX's collectives and lax.ppermute only.
A program may use at most 192 MiB of HBM per device.

```python
import math
import jax
import jax.numpy as jnp
from jax import lax

D = 1024
HEADS = 16
HEAD = 64
FF = 4096
ROWS = 512
MINLEN = 128
SLOTS = 8
MB = 2
BATCH_ROWS = 8192
N_DP = 16


def draw_lengths(key, part):
    first, second, third = jax.random.split(key, 3)
    levels = (ROWS // MINLEN).bit_length() - 1
    power = jax.random.randint(first, (MB, N_DP, SLOTS), 0, levels + 1)
    base = MINLEN * jnp.left_shift(jnp.ones_like(power), power)
    extra = jax.random.randint(second, (MB, N_DP, SLOTS), 0, base)
    drawn = jnp.minimum(base + extra, ROWS)
    used = jax.random.randint(third, (MB, N_DP, 1), 1, SLOTS + 1)
    slot = jnp.arange(SLOTS, dtype=jnp.int32)
    drawn = jnp.where(slot[None, None, :] < used, drawn, 0)
    ends = jnp.minimum(jnp.cumsum(drawn, axis=-1, dtype=jnp.int32), ROWS)
    before = jnp.concatenate([jnp.zeros((MB, N_DP, 1), jnp.int32), ends[..., :-1]], axis=-1)
    lens = (ends - before).astype(jnp.int32)
    whole = jnp.where(slot == 0, ROWS, 0).astype(jnp.int32)
    lens = lens.at[0, 0].set(whole)
    return lens.astype(jnp.int32)


def block_levels(stream_key, shape, cuts, smallest, top_value):
    level, own = 1.0, jax.random.fold_in(stream_key, 6)
    for dim, parts in cuts:
        heights = jnp.exp(jax.random.uniform(jax.random.fold_in(own, dim), (parts,), jnp.float32, smallest / len(cuts), top_value / len(cuts)))
        level = level * jnp.repeat(heights, shape[dim] // parts).reshape([-1 if axis == dim else 1 for axis in range(len(shape))])
    return level


def noise(stream_key, extent, scale, limit, cuts=(), kind=jnp.bfloat16):
    values = scale * jax.random.normal(stream_key, extent, jnp.float32)
    if cuts:
        values = values * block_levels(stream_key, extent, cuts, -0.22, 0.18)
    return jnp.clip(values, -limit, limit).astype(kind)


def setup_inputs(seed: int = 0) -> dict:
    streams_of = jax.random.split(jax.random.key(seed), 18)
    return {
        "inputs": noise(streams_of[0], (MB, BATCH_ROWS, D), 1.0, 6.0, ((1, 32),)),
        "lengths": draw_lengths(jax.random.fold_in(streams_of[17], 71), 0),
        "query_weight": noise(streams_of[2], (D, HEADS * HEAD), D ** -0.5, 0.1875, ((1, 2),)),
        "key_weight": noise(streams_of[3], (D, HEADS * HEAD), D ** -0.5, 0.1875, ((1, 2),)),
        "value_weight": noise(streams_of[4], (D, HEADS * HEAD), D ** -0.5, 0.1875, ((1, 2),)),
        "output_weight": noise(streams_of[5], (HEADS * HEAD, D), (HEADS * HEAD) ** -0.5, 0.1875, ((0, 2),)),
        "inner_weight": noise(streams_of[6], (D, FF), D ** -0.5, 0.1875, ((1, 2),)),
        "outer_weight": noise(streams_of[7], (FF, D), FF ** -0.5, 0.09375, ((0, 2),)),
        "entry_gain": jnp.clip(1.0 + 0.15 * jax.random.normal(streams_of[8], (D,), jnp.float32), 0.25, 1.75),
        "entry_bias": noise(streams_of[9], (D,), 0.5, 3.0, (), jnp.float32),
        "merge_gain": jnp.clip(1.0 + 0.15 * jax.random.normal(streams_of[10], (D,), jnp.float32), 0.25, 1.75),
        "merge_bias": noise(streams_of[11], (D,), 0.5, 3.0, (), jnp.float32),
        "inlet_gain": jnp.clip(1.0 + 0.15 * jax.random.normal(streams_of[12], (D,), jnp.float32), 0.25, 1.75),
        "inlet_bias": noise(streams_of[13], (D,), 0.5, 3.0, (), jnp.float32),
        "outlet_gain": jnp.clip(1.0 + 0.15 * jax.random.normal(streams_of[14], (D,), jnp.float32), 0.25, 1.75),
        "outlet_bias": noise(streams_of[15], (D,), 0.5, 3.0, (), jnp.float32),
        "cotangent": noise(streams_of[16], (MB, BATCH_ROWS, D), 1.0, 6.0, ((1, 32),)),
    }


@jax.custom_vjp
def low(v):
    return lax.optimization_barrier(v.astype(jnp.bfloat16)).astype(jnp.float32)

@jax.custom_vjp
def low_back(v):
    return v

def low_keep(v):
    return (low(v), None)

def low_pass(kept, grad):
    return (grad,)

def back_keep(v):
    return (v, None)

def back_low(kept, grad):
    return (low(grad),)
low.defvjp(low_keep, low_pass)
low_back.defvjp(back_keep, back_low)
NEGATIVE = -1e+30

def layer_norm(values, gain, bias):
    center = values - lax.optimization_barrier(jnp.mean(values, axis=-1, keepdims=True))
    spread = lax.optimization_barrier(jnp.mean(center * center, axis=-1, keepdims=True))
    return center * lax.rsqrt(spread + 1e-05) * gain + bias

def seq_layout(lens):
    ends = jnp.cumsum(lens, dtype=jnp.int32)
    index = jnp.arange(ROWS, dtype=jnp.int32)
    after = index[:, None] >= ends[None, :]
    segment = lax.optimization_barrier(jnp.sum(after.astype(jnp.int32), axis=1)).astype(jnp.int32)
    begin = lax.optimization_barrier(jnp.max(jnp.where(after, ends[None, :], 0), axis=1)).astype(jnp.int32)
    return (segment, (index - begin).astype(jnp.float32))

def rotate(values, cosine, sine):
    half = values.shape[-1] // 2
    first = values[..., :half]
    second = values[..., half:]
    cosine = cosine[..., None, :]
    sine = sine[..., None, :]
    return jnp.concatenate([first * cosine - second * sine, first * sine + second * cosine], axis=-1)

def attend(packed):
    query, keys, values, segment = packed
    scores = jnp.einsum('qhd,khd->hqk', query, keys, precision=lax.Precision.HIGHEST) * 0.125
    scores = low_back(scores)
    index = jnp.arange(ROWS, dtype=jnp.int32)
    allowed = (segment[:, None] == segment[None, :]) & (index[None, :] <= index[:, None])
    scores = jnp.where(allowed[None], scores, NEGATIVE)
    probs = low(jax.nn.softmax(scores, axis=-1))
    return jnp.einsum('hqk,khd->qhd', probs, values, precision=lax.Precision.HIGHEST)

def matmul(left, right):
    return jnp.dot(left, right, precision=lax.Precision.HIGHEST)

def reference(inputs, lengths, query_weight, key_weight, value_weight, output_weight, inner_weight, outer_weight, entry_gain, entry_bias, merge_gain, merge_bias, inlet_gain, inlet_bias, outlet_gain, outlet_bias, cotangent):
    buffers = MB * N_DP
    tokens = buffers * ROWS
    segment, place = jax.vmap(seq_layout)(lengths.reshape(buffers, SLOTS))
    half = HEAD // 2
    rate = jnp.exp(jnp.arange(half, dtype=jnp.float32) * (-math.log(10000.0) / half))
    angle = place[..., None] * rate
    cosine = jnp.cos(angle)
    sine = jnp.sin(angle)

    def forward(start, w_query, w_key, w_value, w_output, w_inner, w_outer, g_entry, b_entry, g_merge, b_merge, g_inlet, b_inlet, g_outlet, b_outlet):
        normed = low(layer_norm(start, g_entry, b_entry))

        def split_heads(weight):
            return low_back(matmul(normed, weight)).reshape(buffers, ROWS, HEADS, HEAD)
        query = low(rotate(split_heads(w_query), cosine, sine))
        keys = low(rotate(split_heads(w_key), cosine, sine))
        values = low(split_heads(w_value))
        attended = lax.map(jax.checkpoint(attend), (query, keys, values, segment))
        attended = low(low_back(attended.reshape(tokens, HEADS * HEAD)))
        branch = low_back(matmul(attended, w_output))
        hidden = start + layer_norm(branch, g_merge, b_merge)
        inlet = low(layer_norm(hidden, g_inlet, b_inlet))
        pre_act = low_back(matmul(inlet, w_inner))
        activated = low(jax.nn.gelu(pre_act, approximate=False))
        second = low_back(matmul(activated, w_outer))
        return hidden + layer_norm(second, g_outlet, b_outlet)
    start = inputs.astype(jnp.float32).reshape(tokens, D)
    result, pull = jax.vjp(forward, start, query_weight.astype(jnp.float32), key_weight.astype(jnp.float32), value_weight.astype(jnp.float32), output_weight.astype(jnp.float32), inner_weight.astype(jnp.float32), outer_weight.astype(jnp.float32), entry_gain, entry_bias, merge_gain, merge_bias, inlet_gain, inlet_bias, outlet_gain, outlet_bias)
    grads = pull(cotangent.astype(jnp.float32).reshape(tokens, D))
    outputs = result.astype(jnp.bfloat16).reshape(inputs.shape)
    input_grad = grads[0].astype(jnp.bfloat16).reshape(inputs.shape)
    return (outputs, input_grad, grads[1], grads[2], grads[3], grads[4], grads[5], grads[6], grads[7], grads[8], grads[9], grads[10], grads[11], grads[12], grads[13], grads[14])
```

```python
import math

import jax
import jax.numpy as jnp
from jax import lax
from jax.sharding import PartitionSpec as P

HEAD = 64


NEGATIVE = -1e30


def layer_norm(values, gain, bias):
    center = values - jnp.mean(values, axis=-1, keepdims=True)
    spread = jnp.mean(center * center, axis=-1, keepdims=True)
    return center * lax.rsqrt(spread + 1e-05) * gain + bias


def exact_gelu(values):
    return jax.nn.gelu(values, approximate=False)


def seq_layout(lens, rows):
    slot = jnp.arange(lens.shape[0], dtype=jnp.int32)
    ends = jnp.sum(jnp.where(slot[None, :] <= slot[:, None], lens[None, :], 0), axis=1)
    index = jnp.arange(rows, dtype=jnp.int32)
    after = index[:, None] >= ends[None, :]
    segment = jnp.sum(after.astype(jnp.int32), axis=1)
    begin = jnp.max(jnp.where(after, ends[None, :], 0), axis=1)
    return (segment, (index - begin).astype(jnp.float32))


def rotary_tables(place, width):
    half = width // 2
    rate = jnp.exp(jnp.arange(half, dtype=jnp.float32) * (-math.log(10000.0) / half))
    angle = place[:, None] * rate[None, :]
    return (jnp.cos(angle)[:, None, :], jnp.sin(angle)[:, None, :])


def rotate(values, cosine, sine):
    half = values.shape[-1] // 2
    first = values[..., :half]
    second = values[..., half:]
    return jnp.concatenate(
        [first * cosine - second * sine, first * sine + second * cosine], axis=-1
    )


def rotate_back(grads, cosine, sine):
    half = grads.shape[-1] // 2
    first = grads[..., :half]
    second = grads[..., half:]
    return jnp.concatenate(
        [first * cosine + second * sine, second * cosine - first * sine], axis=-1
    )


def contract_rows(left, right):
    return lax.dot_general(
        left, right, (((0,), (0,)), ((), ())), preferred_element_type=jnp.float32
    )


def times_transpose(left, right):
    return lax.dot_general(
        left, right, (((1,), (1,)), ((), ())), preferred_element_type=jnp.float32
    )


def masked_scores(query_block, keys, segment, begin, block):
    rows = keys.shape[0]
    scores = (
        jnp.einsum("qhd,khd->hqk", query_block, keys, preferred_element_type=jnp.float32) * 0.125
    )
    query_index = begin + jnp.arange(block, dtype=jnp.int32)
    key_index = jnp.arange(rows, dtype=jnp.int32)
    allowed = (segment[:, None] == segment[None, :]) & (key_index[None, :] <= query_index[:, None])
    return jnp.where(allowed[None], scores, NEGATIVE)


def attend_forward(query, keys, values, segment, block):
    rows = keys.shape[0]

    def one_block(number):
        begin = number * block
        scores = masked_scores(query, keys, segment, begin, block)
        peak = jnp.max(scores, axis=-1, keepdims=True)
        raised = jnp.exp(scores - peak)
        total = jnp.sum(raised, axis=-1, keepdims=True)
        probs = (raised / total).astype(jnp.bfloat16)
        attended = jnp.einsum("hqk,khd->qhd", probs, values, preferred_element_type=jnp.float32)
        return (attended, (peak + jnp.log(total))[..., 0])

    attended, logsum = lax.map(one_block, jnp.arange(rows // block, dtype=jnp.int32))
    return (attended.reshape(rows, query.shape[1], query.shape[2]), logsum)


def attend_backward(query, keys, values, mixed_grad, segment, logsum, block):
    rows = keys.shape[0]

    def one_block(carry, packed):
        keys_acc, values_acc = carry
        number, block_logsum = packed
        begin = number * block
        scores = masked_scores(query, keys, segment, begin, block)
        probs = jnp.exp(scores - block_logsum[..., None])
        prob_grad = jnp.einsum(
            "qhd,khd->hqk", mixed_grad, values, preferred_element_type=jnp.float32
        )
        offset = jnp.sum(probs * prob_grad, axis=-1, keepdims=True)
        score_grad = (probs * (prob_grad - offset)).astype(jnp.bfloat16)
        query_part = (
            jnp.einsum("hqk,khd->qhd", score_grad, keys, preferred_element_type=jnp.float32) * 0.125
        )
        keys_acc = (
            keys_acc
            + jnp.einsum("hqk,qhd->khd", score_grad, query, preferred_element_type=jnp.float32)
            * 0.125
        )
        values_acc = values_acc + jnp.einsum(
            "hqk,qhd->khd",
            probs.astype(jnp.bfloat16),
            mixed_grad,
            preferred_element_type=jnp.float32,
        )
        return ((keys_acc, values_acc), query_part)

    empty = jnp.zeros(keys.shape, jnp.float32)
    numbers = jnp.arange(rows // block, dtype=jnp.int32)
    (keys_grad, values_grad), query_grad = lax.scan(one_block, (empty, empty), (numbers, logsum))
    return (query_grad.reshape(keys.shape), keys_grad, values_grad)


def on_device(
    inputs,
    lengths,
    query_weight,
    key_weight,
    value_weight,
    output_weight,
    inner_weight,
    outer_weight,
    entry_gain,
    entry_bias,
    merge_gain,
    merge_bias,
    inlet_gain,
    inlet_bias,
    outlet_gain,
    outlet_bias,
    cotangent,
):
    groups = lax.axis_size("tensor")
    local_rows = inputs.shape[1]
    rows = local_rows * groups
    width = query_weight.shape[1]
    block = min(512, rows)
    joined = jnp.concatenate([query_weight, key_weight, value_weight], axis=1)
    inner_use, outer_use = (inner_weight, outer_weight)
    joined_acc = jnp.zeros(joined.shape, jnp.float32)
    output_acc = jnp.zeros(output_weight.shape, jnp.float32)
    inner_acc = jnp.zeros(inner_use.shape, jnp.float32)
    outer_acc = jnp.zeros(outer_use.shape, jnp.float32)
    norm_acc = [jnp.zeros(entry_gain.shape, jnp.float32) for index in range(8)]
    result_list = []
    grad_list = []
    for micro in range(inputs.shape[0]):
        segment, place = seq_layout(lengths[micro, 0], rows)
        cosine, sine = rotary_tables(place, HEAD)
        resid = inputs[micro].astype(jnp.float32)
        normed, entry_pull = jax.vjp(layer_norm, resid, entry_gain, entry_bias)
        gathered = lax.all_gather(normed.astype(jnp.bfloat16), "tensor", axis=0, tiled=True)
        projected = jnp.dot(gathered, joined, preferred_element_type=jnp.float32)
        query = rotate(
            projected[:, :width].reshape(rows, width // HEAD, HEAD), cosine, sine
        ).astype(jnp.bfloat16)
        keys = rotate(
            projected[:, width : 2 * width].reshape(rows, width // HEAD, HEAD), cosine, sine
        ).astype(jnp.bfloat16)
        values = projected[:, 2 * width :].reshape(rows, width // HEAD, HEAD).astype(jnp.bfloat16)
        attended, logsum = attend_forward(query, keys, values, segment, block)
        mixed = attended.reshape(rows, width).astype(jnp.bfloat16)
        branch = lax.psum_scatter(
            jnp.dot(mixed, output_weight, preferred_element_type=jnp.float32),
            "tensor",
            scatter_dimension=0,
            tiled=True,
        )
        merged, merge_pull = jax.vjp(layer_norm, branch, merge_gain, merge_bias)
        hidden = resid + merged
        inlet, inlet_pull = jax.vjp(layer_norm, hidden, inlet_gain, inlet_bias)
        inlet_low = inlet.astype(jnp.bfloat16)
        feed = lax.all_gather(inlet_low, "tensor", axis=0, tiled=True)
        pre_act = jnp.dot(feed, inner_use, preferred_element_type=jnp.float32)
        activated, gelu_pull = jax.vjp(exact_gelu, pre_act)
        act_low = activated.astype(jnp.bfloat16)
        second = lax.psum_scatter(
            jnp.dot(act_low, outer_use, preferred_element_type=jnp.float32),
            "tensor",
            scatter_dimension=0,
            tiled=True,
        )
        finished, outlet_pull = jax.vjp(layer_norm, second, outlet_gain, outlet_bias)
        result_list.append((hidden + finished).astype(jnp.bfloat16))
        upstream = cotangent[micro].astype(jnp.float32)
        second_grad, outlet_gain_part, outlet_bias_part = outlet_pull(upstream)
        second_low = second_grad.astype(jnp.bfloat16)
        back_feed = lax.all_gather(second_low, "tensor", axis=0, tiled=True)
        outer_term = contract_rows(act_low, back_feed)
        act_grad = times_transpose(back_feed, outer_use)
        (pre_grad,) = gelu_pull(act_grad)
        pre_low = pre_grad.astype(jnp.bfloat16)
        inner_term = contract_rows(feed, pre_low)
        inlet_grad = lax.psum_scatter(
            times_transpose(pre_low, inner_use), "tensor", scatter_dimension=0, tiled=True
        )
        hidden_part, inlet_gain_part, inlet_bias_part = inlet_pull(inlet_grad)
        hidden_grad = upstream + hidden_part
        branch_grad, merge_gain_part, merge_bias_part = merge_pull(hidden_grad)
        back_mix = lax.all_gather(branch_grad.astype(jnp.bfloat16), "tensor", axis=0, tiled=True)
        output_term = contract_rows(mixed, back_mix)
        mixed_grad = (
            times_transpose(back_mix, output_weight)
            .astype(jnp.bfloat16)
            .reshape(rows, width // HEAD, HEAD)
        )
        query_part, keys_part, values_part = attend_backward(
            query, keys, values, mixed_grad, segment, logsum, block
        )
        projected_grad = jnp.concatenate(
            [
                rotate_back(query_part, cosine, sine).reshape(rows, width),
                rotate_back(keys_part, cosine, sine).reshape(rows, width),
                values_part.reshape(rows, width),
            ],
            axis=1,
        ).astype(jnp.bfloat16)
        joined_term = contract_rows(gathered, projected_grad)
        normed_grad = lax.psum_scatter(
            times_transpose(projected_grad, joined).astype(jnp.bfloat16),
            "tensor",
            scatter_dimension=0,
            tiled=True,
        ).astype(jnp.float32)
        resid_part, entry_gain_part, entry_bias_part = entry_pull(normed_grad)
        grad_list.append((hidden_grad + resid_part).astype(jnp.bfloat16))
        parts = [
            entry_gain_part,
            entry_bias_part,
            merge_gain_part,
            merge_bias_part,
            inlet_gain_part,
            inlet_bias_part,
            outlet_gain_part,
            outlet_bias_part,
        ]
        norm_acc = [total + piece for total, piece in zip(norm_acc, parts)]
        joined_acc = joined_acc + joined_term
        output_acc = output_acc + output_term
        inner_acc = inner_acc + inner_term
        outer_acc = outer_acc + outer_term
    joined_acc, output_acc, inner_acc, outer_acc = lax.psum(
        (joined_acc, output_acc, inner_acc, outer_acc), "dp"
    )
    norm_sums = lax.psum(
        (
            norm_acc[0],
            norm_acc[1],
            norm_acc[2],
            norm_acc[3],
            norm_acc[4],
            norm_acc[5],
            norm_acc[6],
            norm_acc[7],
        ),
        ("dp", "tensor"),
    )
    return (
        jnp.stack(result_list),
        jnp.stack(grad_list),
        joined_acc[:, :width],
        joined_acc[:, width : 2 * width],
        joined_acc[:, 2 * width :],
        output_acc,
        inner_acc,
        outer_acc,
        norm_sums[0],
        norm_sums[1],
        norm_sums[2],
        norm_sums[3],
        norm_sums[4],
        norm_sums[5],
        norm_sums[6],
        norm_sums[7],
    )


def solution(mesh):
    placed = (
        P(None, ("dp", "tensor"), None),
        P(None, "dp", None),
        P(None, "tensor"),
        P(None, "tensor"),
        P(None, "tensor"),
        P("tensor", None),
        P(None, "tensor"),
        P("tensor", None),
        P(),
        P(),
        P(),
        P(),
        P(),
        P(),
        P(),
        P(),
        P(None, ("dp", "tensor"), None),
    )
    return jax.shard_map(
        on_device,
        mesh=mesh,
        in_specs=placed,
        out_specs=(
            P(None, ("dp", "tensor"), None),
            P(None, ("dp", "tensor"), None),
            P(None, "tensor"),
            P(None, "tensor"),
            P(None, "tensor"),
            P("tensor", None),
            P(None, "tensor"),
            P("tensor", None),
            P(),
            P(),
            P(),
            P(),
            P(),
            P(),
            P(),
            P(),
        ),
        check_vma=False,
    )
```

```python
import functools
import math

import jax
import jax.numpy as jnp
from jax import lax
from jax.experimental import pallas as pl
from jax.experimental.pallas import tpu as pltpu
from jax.sharding import PartitionSpec as P

HEAD = 64
PAIR = 128
COST = 2 * 10**10
NEGATIVE = -1e30
F32 = jnp.float32
BF16 = jnp.bfloat16
SWAP = [(0, 1), (1, 0)]


def dot(left, right):
    return jnp.dot(left, right, preferred_element_type=F32)


def dot_rows(left, right):
    return lax.dot_general(left, right, (((0,), (0,)), ((), ())), preferred_element_type=F32)


def dot_t(left, right):
    return lax.dot_general(left, right, (((1,), (1,)), ((), ())), preferred_element_type=F32)


def norm_parts(values):
    center = values - jnp.mean(values, axis=-1, keepdims=True)
    scale = lax.rsqrt(jnp.mean(center * center, axis=-1, keepdims=True) + 1e-05)
    return center * scale, scale


def norm_back(grads, unit, scale, gain):
    inner = grads * gain
    first = jnp.mean(inner, axis=-1, keepdims=True)
    second = jnp.mean(inner * unit, axis=-1, keepdims=True)
    below = scale * (inner - first - unit * second)
    return (
        below,
        jnp.sum(grads * unit, axis=0, keepdims=True),
        jnp.sum(grads, axis=0, keepdims=True),
    )


def partner_of(values):
    lane = lax.broadcasted_iota(jnp.int32, values.shape, 1)
    return jnp.where((lane & 63) < 32, pltpu.roll(values, 96, 1), pltpu.roll(values, 32, 1))


def half_mask(values, which):
    lane = lax.broadcasted_iota(jnp.int32, values.shape, 1)
    keep = (lane < HEAD) if which == 0 else (lane >= HEAD)
    return jnp.where(keep, values, jnp.zeros_like(values))


def segments(ends_ref, shape, dim):
    index = lax.broadcasted_iota(jnp.int32, shape, dim)
    total = jnp.zeros(shape, jnp.int32)
    for slot in range(ends_ref.shape[0]):
        total = total + (index >= ends_ref[slot]).astype(jnp.int32)
    return index, total


def write_rows(core_ref, own_ref, other_ref, dest_ref):
    half = own_ref.shape[0]
    mine = pl.multiple_of(core_ref[0] * half, half)
    theirs = pl.multiple_of((1 - core_ref[0]) * half, half)
    dest_ref[pl.ds(mine, half), :] = own_ref[...]
    dest_ref[pl.ds(theirs, half), :] = other_ref[...]


def heads_forward(a, wq_ref, wk_ref, wv_ref, cos, sin, bias_ref, q_ref, k_ref, v_ref, o_ref):
    rows, width = q_ref.shape
    half = rows // 2
    wide = 256
    for tile in range(width // wide):
        span = slice(tile * wide, (tile + 1) * wide)
        ql = dot(a, wq_ref[:, span])
        kl = dot(a, wk_ref[:, span])
        vl = dot(a, wv_ref[:, span])
        for part in range(wide // PAIR):
            at = slice(part * PAIR, (part + 1) * PAIR)
            to = slice(tile * wide + part * PAIR, tile * wide + (part + 1) * PAIR)
            u = ql[:, at]
            q_ref[:, to] = (u * cos + partner_of(u) * sin).astype(BF16) * jnp.asarray(0.125, BF16)
            u = kl[:, at]
            k_ref[:, to] = (u * cos + partner_of(u) * sin).astype(BF16)
            v_ref[:, to] = vl[:, at].astype(BF16)
    for pair in range(width // PAIR):
        to = slice(pair * PAIR, (pair + 1) * PAIR)
        keys = k_ref[:, to]
        values = v_ref[:, to]
        masked = [(half_mask(keys, w), half_mask(values, w)) for w in range(2)]
        for block in range(2):
            at = slice(block * half, (block + 1) * half)
            reach = (block + 1) * half
            query = q_ref[at, to]
            total = jnp.zeros((half, PAIR), F32)
            for km, vm in masked:
                s = dot_t(query, km[:reach]) + bias_ref[at, :reach]
                s = jnp.exp(s - jnp.max(s, axis=-1, keepdims=True))
                p = (s * (1.0 / jnp.sum(s, axis=-1, keepdims=True))).astype(BF16)
                total = total + dot(p, vm[:reach])
            o_ref[at, to] = total.astype(BF16)


def fill_bias(ends_ref, bias_ref, keys_first):
    rows = bias_ref.shape[0]
    row_index, row_segment = segments(ends_ref, (rows, 1), 0)
    lane_index, lane_segment = segments(ends_ref, (1, rows), 1)
    if keys_first:
        allowed = (row_segment == lane_segment) & (row_index <= lane_index)
    else:
        allowed = (row_segment == lane_segment) & (lane_index <= row_index)
    bias_ref[...] = jnp.where(allowed, 0.0, NEGATIVE)


def first_heads(core, ends, own, other, gain, bias, cos, sin, wq, wk, wv, a_out, q, k, v, o, x_s, mask_s):
    write_rows(core, own, other, x_s)
    unit, _ = norm_parts(x_s[...].astype(F32))
    a_out[...] = (unit * gain[...] + bias[...]).astype(BF16)
    fill_bias(ends, mask_s, False)
    heads_forward(a_out[...], wq, wk, wv, cos[...], sin[...], mask_s, q, k, v, o)


def second_heads(
    core, ends, own, other, a, cos, sin, wq, wk, wv, o_first, wo_first, wo,
    merge_gain, merge_bias, inlet_gain, inlet_bias,
    q, k, v, o, z_out, h_out, c_out, x_s, mask_s,
):
    write_rows(core, own, other, x_s)
    fill_bias(ends, mask_s, False)
    heads_forward(a[...], wq, wk, wv, cos[...], sin[...], mask_s, q, k, v, o)
    z = dot(o_first[...], wo_first[...]) + dot(o[...], wo[...])
    z_out[...] = z
    unit, _ = norm_parts(z)
    h = x_s[...].astype(F32) + (unit * merge_gain[...] + merge_bias[...])
    h_out[...] = h
    unit, _ = norm_parts(h)
    c_out[...] = (unit * inlet_gain[...] + inlet_bias[...]).astype(BF16)


def gelu_parts(f):
    x = jnp.abs(f) * 0.7071067811865476
    t = 1.0 / (1.0 + 0.3275911 * x)
    poly = t * (0.254829592 + t * (-0.284496736 + t * (1.421413741 + t * (-1.453152027 + t * 1.061405429))))
    bell = jnp.exp(-x * x)
    tail = 0.5 * poly * bell
    phi = jnp.where(f >= 0, 1.0 - tail, tail)
    return f * phi, phi + f * (0.3989422804014327 * bell)


def units_forward(c, wi, wo, e_out, slope_out):
    f = dot(c, wi)
    e, slope = gelu_parts(f)
    e = e.astype(BF16)
    e_out[...] = e
    slope_out[...] = slope.astype(BF16)
    return dot(e, wo)


def first_units(c, wi, wo, e_out, slope_out, n_out):
    part = units_forward(c[...], wi[...], wo[...], e_out, slope_out)
    step = pl.program_id(0)

    @pl.when(step == 0)
    def _():
        n_out[...] = part

    @pl.when(step > 0)
    def _():
        n_out[...] += part


def second_units(core, c, wi, wo, n_first, h, cot_own, cot_other, gain, bias,
                 e_out, slope_out, y_out, n_grad, gain_out, bias_out, n_s, y_s):
    part = units_forward(c[...], wi[...], wo[...], e_out, slope_out)
    step = pl.program_id(0)

    @pl.when(step == 0)
    def _():
        n_s[...] = n_first[...] + part

    @pl.when(step > 0)
    def _():
        n_s[...] += part

    @pl.when(step == pl.num_programs(0) - 1)
    def _():
        write_rows(core, cot_own, cot_other, y_s)
        unit, scale = norm_parts(n_s[...])
        y_out[...] = (h[...] + (unit * gain[...] + bias[...])).astype(BF16)
        below, gains, biases = norm_back(y_s[...].astype(F32), unit, scale, gain[...])
        n_grad[...] = below.astype(BF16)
        gain_out[...] = gains
        bias_out[...] = biases


def outer_terms(e, n_grad, out):
    out[...] = dot_rows(e[...], n_grad[...]).astype(BF16)


def units_back(n_grad, c, wi, wo, slope, inner_out):
    f_grad = (dot_t(n_grad[...], wo[...]) * slope[...].astype(F32)).astype(BF16)
    inner_out[0] = dot_rows(c[...], f_grad).astype(BF16)
    return dot_t(f_grad, wi[...])


def first_units_back(n_grad, c, wi, wo, slope, inner_out, c_grad):
    part = units_back(n_grad, c, wi, wo, slope, inner_out)
    step = pl.program_id(0)

    @pl.when(step == 0)
    def _():
        c_grad[...] = part

    @pl.when(step > 0)
    def _():
        c_grad[...] += part


def more_units_back(n_grad, c, wi, wo, slope, c_before, inner_out, c_grad):
    part = units_back(n_grad, c, wi, wo, slope, inner_out)
    step = pl.program_id(0)

    @pl.when(step == 0)
    def _():
        c_grad[...] = c_before[...] + part

    @pl.when(step > 0)
    def _():
        c_grad[...] += part


def last_units_back(core, n_grad, c, wi, wo, slope, c_first, cot_own, cot_other, h, z, inlet_gain, merge_gain,
                    inner_out, h_grad, z_grad, sums_out, c_s, y_s):
    part = units_back(n_grad, c, wi, wo, slope, inner_out)
    step = pl.program_id(0)

    @pl.when(step == 0)
    def _():
        c_s[...] = c_first[...] + part

    @pl.when(step > 0)
    def _():
        c_s[...] += part

    @pl.when(step == pl.num_programs(0) - 1)
    def _():
        write_rows(core, cot_own, cot_other, y_s)
        unit, scale = norm_parts(h[...])
        below, inlet_gains, inlet_biases = norm_back(c_s[...], unit, scale, inlet_gain[...])
        h_part = y_s[...].astype(F32) + below
        h_grad[...] = h_part
        unit, scale = norm_parts(z[...])
        below, merge_gains, merge_biases = norm_back(h_part, unit, scale, merge_gain[...])
        z_grad[...] = below.astype(BF16)
        sums_out[0:1, :] = merge_gains
        sums_out[1:2, :] = merge_biases
        sums_out[2:3, :] = inlet_gains
        sums_out[3:4, :] = inlet_biases


def heads_back(ends, z_grad, a, cos, sin, wq, wk, wv, wo, q, k, v, o,
               qk_out, vo_out, mask_s, ql_s, kl_s, vl_s, o_s):
    rows, width = q.shape
    half = rows // 2
    fill_bias(ends, mask_s, True)
    o_s[...] = dot_t(z_grad[...], wo[...]).astype(BF16)
    for part in range(2):
        at = slice(part * width, (part + 1) * width)
        vo_out[1, at, :] = dot_rows(o[...], z_grad[:, at]).astype(BF16)
    cosine, sine = cos[...], sin[...]
    for pair in range(width // PAIR):
        to = slice(pair * PAIR, (pair + 1) * PAIR)
        query, keys, values, mixed = q[:, to], k[:, to], v[:, to], o_s[:, to]
        key_acc = [jnp.zeros((half, PAIR), F32) for _ in range(2)]
        value_acc = [jnp.zeros((half, PAIR), F32) for _ in range(2)]
        query_acc = [jnp.zeros((half, PAIR), F32) for _ in range(2)]
        for which in range(2):
            qm, km, vm, om = (half_mask(t, which) for t in (query, keys, values, mixed))
            for block in range(2):
                at = slice(block * half, (block + 1) * half)
                reach = (block + 1) * half
                s = dot_t(km[:reach], query[at]) + mask_s[:reach, at]
                s = jnp.exp(s - jnp.max(s, axis=0, keepdims=True))
                p = s * (1.0 / jnp.sum(s, axis=0, keepdims=True))
                grown = dot_t(vm[:reach], mixed[at])
                offset = jnp.sum(p * grown, axis=0, keepdims=True)
                ds = (p * (grown - offset)).astype(BF16)
                p = p.astype(BF16)
                query_acc[block] = query_acc[block] + dot_rows(ds, km[:reach])
                for piece in range(block + 1):
                    rs = slice(piece * half, (piece + 1) * half)
                    key_acc[piece] = key_acc[piece] + dot(ds[rs], qm[at])
                    value_acc[piece] = value_acc[piece] + dot(p[rs], om[at])
        for block in range(2):
            at = slice(block * half, (block + 1) * half)
            u = query_acc[block] * 0.125
            ql_s[at, to] = (u * cosine[at] - partner_of(u) * sine[at]).astype(BF16)
            u = key_acc[block]
            kl_s[at, to] = (u * cosine[at] - partner_of(u) * sine[at]).astype(BF16)
            vl_s[at, to] = value_acc[block].astype(BF16)
    a_all = a[...]
    qk_out[0] = dot_rows(a_all, ql_s[...]).astype(BF16)
    qk_out[1] = dot_rows(a_all, kl_s[...]).astype(BF16)
    vo_out[0] = dot_rows(a_all, vl_s[...]).astype(BF16)
    return dot_t(ql_s[...], wq[...]) + dot_t(kl_s[...], wk[...]) + dot_t(vl_s[...], wv[...])


def first_heads_back(ends, z_grad, a, cos, sin, wq, wk, wv, wo, q, k, v, o,
                     qk_out, vo_out, a_grad, *scratch):
    a_grad[...] = heads_back(ends, z_grad, a, cos, sin, wq, wk, wv, wo, q, k, v, o,
                             qk_out, vo_out, *scratch)


def second_heads_back(core, ends, z_grad, a, cos, sin, wq, wk, wv, wo, q, k, v, o, a_first, own, other, h_grad, gain,
                      qk_out, vo_out, x_grad, gain_out, bias_out, *scratch):
    *scratch, x_s = scratch
    a_grad = a_first[...] + heads_back(ends, z_grad, a, cos, sin, wq, wk, wv, wo, q, k, v, o,
                                       qk_out, vo_out, *scratch)
    write_rows(core, own, other, x_s)
    unit, scale = norm_parts(x_s[...].astype(F32))
    below, gains, biases = norm_back(a_grad, unit, scale, gain[...])
    x_grad[...] = (h_grad[...] + below).astype(BF16)
    gain_out[...] = gains
    bias_out[...] = biases


SMEM = pl.BlockSpec(memory_space=pltpu.SMEM)
FULL = pl.BlockSpec(memory_space=pltpu.VMEM)


def params(limit, **kw):
    return pltpu.CompilerParams(vmem_limit_bytes=limit * 2**20, **kw)


def shape(dims, kind=BF16):
    return jax.ShapeDtypeStruct(dims, kind)


def call(kernel, operands, outs, scratch, smem, limit):
    return pl.pallas_call(
        kernel,
        in_specs=[SMEM] * smem + [FULL] * (len(operands) - smem),
        out_specs=[FULL] * len(outs),
        out_shape=outs,
        scratch_shapes=scratch,
        compiler_params=params(limit),
        cost_estimate=pl.CostEstimate(flops=COST, bytes_accessed=2**20, transcendentals=0),
    )(*operands)


def tiled(kernel, operands, kinds, outs, out_kinds, scratch, tile, steps, limit, first=0):
    def spec(kind, dims, first=0):
        if kind == "s":
            return SMEM
        if kind == "f":
            return pl.BlockSpec(dims, lambda i: (0,) * len(dims))
        if kind == "3":
            return pl.BlockSpec((1, *dims[1:]), lambda i: (i, 0, 0))
        if kind == "c":
            return pl.BlockSpec((dims[0], tile), lambda i: (0, i + first))
        return pl.BlockSpec((tile, dims[1]), lambda i: (i + first, 0))
    return pl.pallas_call(
        kernel,
        grid=(steps,),
        in_specs=[spec(kind, op.shape, first) for kind, op in zip(kinds, operands)],
        out_specs=[spec(kind, out.shape) for kind, out in zip(out_kinds, outs)],
        out_shape=outs,
        scratch_shapes=scratch,
        compiler_params=params(limit, dimension_semantics=("arbitrary",)),
        cost_estimate=pl.CostEstimate(flops=COST, bytes_accessed=2**20, transcendentals=0),
    )(*operands)


def coordinates(mesh):
    total = mesh.shape["dp"]
    places = [getattr(d, "coords", None) for d in mesh.devices.reshape(total, -1)[:, 0]]
    if all(p is not None and len(p) == 3 for p in places):
        sizes = [len({p[i] for p in places}) for i in range(3)]
        low = [min(p[i] for p in places) for i in range(3)]
        order = [((p[2] - low[2]) * sizes[1] + p[1] - low[1]) * sizes[0] + p[0] - low[0] for p in places]
        if order == list(range(total)):
            return tuple(sizes)
    return (2, 2, total // 4) if total % 4 == 0 else (1, 1, total)


def add(*terms):
    total = terms[0].astype(F32)
    for term in terms[1:]:
        total = total + term.astype(F32)
    return total.astype(BF16)


def trade(value, bit):
    return lax.ppermute(value, "dp", [(i, i ^ bit) for i in range(lax.axis_size("dp"))])


class Line:
    def __init__(self, token):
        self.token = token

    def fence(self, values):
        self.token, values = lax.optimization_barrier((self.token, values))
        return values

    def done(self, value):
        self.token = value
        return value


def settle_kernel(count, spots, *refs):
    *pieces, out = refs
    pieces = pieces[-4:]
    step = pl.program_id(0)
    size = pieces[0].shape[0]
    per = 4 // count
    for i, piece in enumerate(pieces):
        if count == 1:
            out[pl.ds(pl.multiple_of(spots[i] * size, size), size), :] = piece[...].astype(F32)
        else:
            @pl.when(spots[i] // per == step)
            def _():
                at = spots[i] % per
                out[pl.ds(pl.multiple_of(at * size, size), size), :] = piece[...].astype(F32)


def settle(spots, pieces, whole, dims, blocks, count):
    lines, columns = 4 * pieces[0].shape[0] // count, pieces[0].shape[1]
    before = [] if whole is None else [whole]
    base, last = blocks[0], blocks[-1]
    return pl.pallas_call(
        functools.partial(settle_kernel, count),
        grid=(count,),
        in_specs=[SMEM] + [pl.BlockSpec(memory_space=pl.ANY)] * len(before)
        + [pl.BlockSpec(p.shape, lambda i: (0, 0)) for p in pieces],
        out_specs=pl.BlockSpec((lines, columns), lambda i: (base[0], base[1] + i)),
        out_shape=shape(dims, F32),
        input_output_aliases={1: 0} if before else {},
        compiler_params=pltpu.CompilerParams(vmem_limit_bytes=20 * 2**20),
        cost_estimate=pl.CostEstimate(flops=COST, bytes_accessed=2**20, transcendentals=0),
    )(spots, *before, *pieces)


def settle_heads_kernel(folded, spots, *refs):
    pieces, (top, bottom) = refs[:4], refs[4:]
    size = pieces[0].shape[0]
    for i, piece in enumerate(pieces):
        for spot in range(4):
            @pl.when(spots[i] == spot)
            def _():
                at = spot % 2
                if spot < 2:
                    top[at * size:(at + 1) * size, :] = piece[...].astype(F32)
                elif folded:
                    bottom[:, at * size:(at + 1) * size] = piece[...].astype(F32)
                else:
                    bottom[at * size:(at + 1) * size, :] = piece[...].astype(F32)


def settle_heads(spots, pieces, folded):
    lines, columns = pieces[0].shape
    return pl.pallas_call(
        functools.partial(settle_heads_kernel, folded),
        in_specs=[SMEM] + [FULL] * 4,
        out_specs=[FULL, FULL],
        out_shape=[shape((2 * lines, columns), F32), shape((lines, 2 * columns) if folded else (2 * lines, columns), F32)],
        compiler_params=pltpu.CompilerParams(vmem_limit_bytes=12 * 2**20),
        cost_estimate=pl.CostEstimate(flops=COST, bytes_accessed=2**20, transcendentals=0),
    )(spots, *pieces)


class Chunk:
    def __init__(self, line, here, core, own, peer, finish):
        self.line, self.finish = line, finish
        self.own, self.other = own, swap(peer)
        self.a, self.z, self.b = jnp.where(core == 0, here[1], here[2]), here[4], jnp.where(core == 0, here[2], here[1])

    def part(self, value, *picks):
        value = value.reshape(*([2] * len(picks)), -1, value.shape[-1])
        for p in picks:
            value = lax.dynamic_index_in_dim(value, p, 0, keepdims=False)
        return value

    def trade(self, value, *bits):
        pairs = [(2 * i + c, 2 * (i ^ bits[c]) + c) for i in range(lax.axis_size("dp")) for c in range(2)]
        return lax.ppermute(value, ("dp", "tensor"), pairs)

    def step(self, number):
        getattr(self, f"step{number}")()

    def step0(self):
        own, other = self.line.fence((self.own, self.other))
        send = self.line.done(add(self.part(own, 1 - self.a), self.part(other, 1 - self.a)))
        self.first = self.trade(send, 1, 2)

    def step1(self):
        own, other, first = self.line.fence((self.own, self.other, self.first))
        a, z = self.a, 1 - self.z
        send = self.line.done(add(self.part(own, a, z), self.part(other, a, z), self.part(first, z)))
        self.second = self.trade(send, 4, 4)

    def step2(self):
        own, other, first, second = self.line.fence((self.own, self.other, self.first, self.second))
        a, z, b = self.a, self.z, 1 - self.b
        send = self.line.done(add(self.part(own, a, z, b), self.part(other, a, z, b), self.part(first, z, b), self.part(second, b)))
        self.third = self.trade(send, 2, 1)

    def step3(self):
        own, other, first, second, third = self.line.fence((self.own, self.other, self.first, self.second, self.third))
        a, z, b = self.a, self.z, self.b
        self.kept = self.line.done(add(self.part(own, a, z, b), self.part(other, a, z, b), self.part(first, z, b),
                                       self.part(second, b), third))
        self.fourth = self.trade(self.kept, 8, 8)

    def step4(self):
        kept, fourth = self.line.fence((self.kept, self.fourth))
        self.total = self.line.done(add(kept, fourth))
        self.fifth = self.trade(self.total, 2, 1)

    def step5(self):
        total, fifth = self.line.fence((self.total, self.fifth))
        low = self.b == 0
        self.mine = self.line.done(jnp.concatenate([jnp.where(low, total, fifth), jnp.where(low, fifth, total)], axis=0))
        self.sixth = self.trade(self.mine, 4, 4)
        self.near = self.trade(self.mine, 1, 2)

    def step6(self):
        self.sixth = self.line.done(self.line.fence(self.sixth))
        self.far = self.trade(self.sixth, 1, 2)

    def step7(self):
        pieces = self.line.fence((self.mine, self.sixth, self.near, self.far))
        a, z = self.a, self.z
        spots = jnp.stack([2 * a + z, 2 * a + 1 - z, 2 * (1 - a) + z, 2 * (1 - a) + 1 - z])
        self.line.done(self.finish(spots, pieces))


def reduce_norms(values, total):
    values = values + swap(values)
    if total & (total - 1):
        return lax.psum(values, "dp")
    bit = 1
    while bit < total:
        values = values + trade(values, bit)
        bit *= 2
    return values


ORDER = (
    "G00", "G01", "G10", "o00", "G11", "o10", "K00", "o01", "K01", "i00", "o11", "o02", "K10", "i01",
    "o12", "o03", "K11", "i10", "i02", "o13", "o04", "H0", "i11", "i03", "o14", "o05", "H1", "h00",
    "h10", "i12", "i04", "o15", "h01", "o06", "h11", "i13", "i05", "o16", "h02", "o07", "h12", "o17",
    "h03", "h13", "i14", "i06", "i15", "h04", "i07", "h14", "h05", "i16", "h15", "h06", "i17", "h16",
    "h07", "h17",
)

LIMITS = {"a1": 12, "a2": 16, "u1": 12, "u2": 24, "g": 12, "k": 16, "l": 20, "h1": 20, "h2": 20}


def swap(value):
    return lax.ppermute(value, "tensor", SWAP)


def on_device(
    sizes, inputs, lengths, query_weight, key_weight, value_weight, output_weight, inner_weight, outer_weight,
    entry_gain, entry_bias, merge_gain, merge_bias, inlet_gain, inlet_bias, outlet_gain, outlet_bias, cotangent,
):
    core = lax.axis_index("tensor").astype(jnp.int32)
    core_s = core.reshape(1)
    half = inputs.shape[1]
    rows = 2 * half
    width = query_weight.shape[1]
    units = inner_weight.shape[1]
    feats = inputs.shape[2]
    row = lambda v: v.reshape(1, feats)
    pick = lambda v, i: lax.dynamic_index_in_dim(v, i, 0, keepdims=False)
    x_own = pick(inputs, core)
    x_other = swap(pick(inputs, 1 - core))
    wq2, wk2, wv2 = swap(query_weight), swap(key_weight), swap(value_weight)
    wo2, wi2, wf2 = swap(output_weight), swap(inner_weight), swap(outer_weight)
    y_own = pick(cotangent, core)
    y_other = swap(pick(cotangent, 1 - core))

    lens = pick(lengths, core)[0]
    slot = jnp.arange(lens.shape[0], dtype=jnp.int32)
    ends = jnp.sum(jnp.where(slot[None, :] <= slot[:, None], lens[None, :], 0), axis=1)
    index = jnp.arange(rows, dtype=jnp.int32)
    begin = jnp.max(jnp.where(index[:, None] >= ends[None, :], ends[None, :], 0), axis=1)
    place = (index - begin).astype(F32)
    lane = jnp.arange(PAIR, dtype=jnp.int32)
    rate = jnp.exp((lane % (HEAD // 2)).astype(F32) * (-math.log(10000.0) / (HEAD // 2)))
    angle = place[:, None] * rate[None, :]
    cos = jnp.cos(angle)
    sin = jnp.sin(angle) * jnp.where(lane % HEAD < HEAD // 2, -1.0, 1.0)[None, :]

    act = shape((rows, width))
    mask = pltpu.VMEM((rows, rows), F32)
    xbuf = pltpu.VMEM((rows, feats), BF16)
    a, q1, k1, v1, o1 = call(
        first_heads,
        [core_s, ends, x_own, x_other, row(entry_gain), row(entry_bias), cos, sin, query_weight, key_weight, value_weight],
        [shape((rows, feats)), act, act, act, act], [xbuf, mask], 2, LIMITS["a1"])
    q2, k2, v2, o2, z, h, c = call(
        second_heads,
        [core_s, ends, x_own, x_other, a, cos, sin, wq2, wk2, wv2, o1, output_weight, wo2,
         row(merge_gain), row(merge_bias), row(inlet_gain), row(inlet_bias)],
        [act, act, act, act, shape((rows, feats), F32), shape((rows, feats), F32), shape((rows, feats))],
        [xbuf, mask], 2, LIMITS["a2"])
    tile = 512
    steps = units // tile
    big = shape((rows, units))
    e1, s1, n1 = tiled(first_units, [c, inner_weight, outer_weight], "fcr",
                       [big, big, shape((rows, feats), F32)], "ccf", [], tile, steps, LIMITS["u1"])
    e2, s2, y, n_grad, outlet_gains, outlet_biases = tiled(
        second_units, [core_s, c, wi2, wf2, n1, h, y_own, y_other, row(outlet_gain), row(outlet_bias)], "sfcrffffff",
        [big, big, shape((rows, feats)), shape((rows, feats)), shape((1, feats), F32), shape((1, feats), F32)], "ccffff",
        [pltpu.VMEM((rows, feats), F32), xbuf], tile, steps, LIMITS["u2"])
    total = shape((rows, feats), F32)
    line = Line(n_grad)
    made = {"c": None}
    wholes = {}
    scratch = [mask] + [pltpu.VMEM((rows, width), BF16)] * 4
    grads = [shape((2, feats, width)), shape((2, feats, width))]

    def outer_step(pair, mine):
        e_in, n_in = line.fence(((e2, e1)[mine], n_grad))
        (out,) = tiled(outer_terms, [e_in, n_in], "cf", [shape((2 * tile, feats))], "r", [], 2 * tile, 1, LIMITS["g"], pair)
        line.done(out)
        return [out]

    def inner_step(pair, mine):
        operands = line.fence([n_grad, c, *((wi2, wf2, s2), (inner_weight, outer_weight, s1))[mine]])
        outs = [shape((2, feats, tile)), total]
        at = (0, 2 * pair)[1]
        if made["c"] is None:
            out, made["c"] = tiled(first_units_back, operands, "ffcrc", outs, "3f", [], tile, 2, LIMITS["k"], at)
        elif pair == steps // 2 - 1 and mine:
            out, made["h"], made["z"], made["sums"] = tiled(
                last_units_back,
                [core_s, *operands, made["c"], y_own, y_other, h, z, row(inlet_gain), row(merge_gain)], "sffcrcfffffff",
                [outs[0], total, shape((rows, feats)), shape((4, feats), F32)], "3fff",
                [pltpu.VMEM((rows, feats), F32), xbuf], tile, 2, LIMITS["l"], at)
        else:
            out, made["c"] = tiled(more_units_back, [*operands, made["c"]], "ffcrcf", outs, "3f", [], tile, 2, LIMITS["k"], at)
        line.done(out)
        return [out.reshape(2 * feats, tile)]

    def heads_step(mine):
        z_grad = line.fence(made["z"])
        if not mine:
            qk, vo, made["a"] = call(
                first_heads_back, [ends, z_grad, a, cos, sin, wq2, wk2, wv2, wo2, q2, k2, v2, o2],
                grads + [total], scratch, 1, LIMITS["h1"])
        else:
            qk, vo, made["x"], made["gain"], made["bias"] = call(
                second_heads_back,
                [core_s, ends, z_grad, a, cos, sin, query_weight, key_weight, value_weight, output_weight, q1, k1, v1, o1,
                 made["a"], x_own, x_other, made["h"], row(entry_gain)],
                grads + [shape((rows, feats)), shape((1, feats), F32), shape((1, feats), F32)], scratch + [xbuf], 2, LIMITS["h2"])
        line.done(qk)
        return [qk.reshape(2 * feats, width), vo.reshape(2 * feats, width)]

    chips = lax.axis_size("dp")
    place_of = lax.axis_index("dp").astype(jnp.int32)
    here = {bit: (place_of // bit) % 2 for bit in (1, 2, 4, 8)}
    outs = {"o": (units, feats), "i": (feats, units)}

    def finisher(name):
        kind, number = name[0], int(name[1])

        def finish(spots, pieces):
            if kind == "o":
                wholes["o"] = settle(spots, pieces, wholes.get("o"), outs["o"], [(number, 0)], 1)
                return wholes["o"]
            if kind == "i":
                wholes["i"] = settle(spots, pieces, wholes.get("i"), outs["i"], [(0, 2 * number), (0, 2 * number + 1)], 2)
                return wholes["i"]
            wholes[name] = settle_heads(spots, pieces, number == 1)
            return wholes[name][1]
        return finish

    halves = {}
    chunks = {}
    fast = tuple(sizes) == (2, 2, 4)

    def ready(name, own, peer):
        if fast:
            chunks[name] = Chunk(line, here, core, own, peer, finisher(name))
        else:
            wholes[name] = lax.psum(add(own, swap(peer)), "dp").astype(F32)

    for what in ORDER:
        name, number = what[:-1], int(what[-1])
        if name[0] in "GK":
            which = int(name[1])
            made_now = (outer_step if name[0] == "G" else inner_step)(which, number)
            key = ("o" if name[0] == "G" else "i") + str(which)
            if number == 0:
                halves[key] = made_now
            else:
                ready(key, made_now[0], halves[key][0])
        elif name == "H":
            made_now = heads_step(number)
            if number == 0:
                halves["h"] = made_now
            else:
                for i in range(2):
                    ready("h" + str(i), made_now[i], halves["h"][i])
        elif fast:
            chunks[name].step(number)
    x_grad, entry_gains, entry_biases, sums = made["x"], made["gain"], made["bias"], made["sums"]

    def spread(full):
        parts = full.reshape(2, half, feats)
        mine = pick(parts, core)
        other = swap(pick(parts, 1 - core))
        first = core == 0
        return jnp.stack([jnp.where(first, mine, other), jnp.where(first, other, mine)])

    outputs = spread(y)
    input_grad = spread(x_grad)
    if not fast:
        wholes["o"] = jnp.concatenate([wholes["o" + str(i)] for i in range(steps // 2)], axis=0)
        wholes["i"] = jnp.concatenate(
            [half for i in range(steps // 2) for half in jnp.split(wholes["i" + str(i)], 2, axis=0)], axis=1)
        wholes["h0"] = jnp.split(wholes["h0"], 2, axis=0)
        value, folded = jnp.split(wholes["h1"], 2, axis=0)
        wholes["h1"] = [value, jnp.concatenate([folded[:width], folded[width:]], axis=1)]
    query_grad, key_grad = wholes["h0"]
    value_grad, output_grad = wholes["h1"]
    inner_grad, outer_grad = wholes["i"], wholes["o"]
    weight_grads = [query_grad, key_grad, value_grad, output_grad, inner_grad, outer_grad]
    norms = [entry_gains, entry_biases, sums[0:1], sums[1:2], sums[2:3], sums[3:4], outlet_gains, outlet_biases]
    norms = reduce_norms(jnp.concatenate(norms, axis=0), chips)
    return (outputs, input_grad, *weight_grads, *[norms[i] for i in range(8)])


def solution(mesh):
    rows = P(None, ("dp", "tensor"), None)
    columns, lines = P(None, "tensor"), P("tensor", None)
    weights = (columns, columns, columns, lines, columns, lines)
    return jax.shard_map(
        functools.partial(on_device, coordinates(mesh)),
        mesh=mesh,
        in_specs=(rows, P(None, "dp", None), *weights, *([P()] * 8), rows),
        out_specs=(rows, rows, *weights, *([P()] * 8)),
        check_vma=False,
    )
```

```python
import functools
import math

import jax
import jax.numpy as jnp
from jax import lax
from jax.experimental import pallas as pl
from jax.experimental.pallas import tpu as pltpu
from jax.sharding import PartitionSpec as P

HEAD = 64
PAIR = 128
COST = 2 * 10**10
NEGATIVE = -1e30
F32 = jnp.float32
BF16 = jnp.bfloat16
SWAP = [(0, 1), (1, 0)]


def dot(left, right):
    return jnp.dot(left, right, preferred_element_type=F32)


def dot_rows(left, right):
    return lax.dot_general(left, right, (((0,), (0,)), ((), ())), preferred_element_type=F32)


def dot_t(left, right):
    return lax.dot_general(left, right, (((1,), (1,)), ((), ())), preferred_element_type=F32)


def norm_parts(values):
    center = values - jnp.mean(values, axis=-1, keepdims=True)
    scale = lax.rsqrt(jnp.mean(center * center, axis=-1, keepdims=True) + 1e-05)
    return center * scale, scale


def norm_back(grads, unit, scale, gain):
    inner = grads * gain
    first = jnp.mean(inner, axis=-1, keepdims=True)
    second = jnp.mean(inner * unit, axis=-1, keepdims=True)
    below = scale * (inner - first - unit * second)
    return (
        below,
        jnp.sum(grads * unit, axis=0, keepdims=True),
        jnp.sum(grads, axis=0, keepdims=True),
    )


def partner_of(values):
    lane = lax.broadcasted_iota(jnp.int32, values.shape, 1)
    return jnp.where((lane & 63) < 32, pltpu.roll(values, 96, 1), pltpu.roll(values, 32, 1))


def half_mask(values, which):
    lane = lax.broadcasted_iota(jnp.int32, values.shape, 1)
    keep = (lane < HEAD) if which == 0 else (lane >= HEAD)
    return jnp.where(keep, values, jnp.zeros_like(values))


def segments(ends_ref, shape, dim):
    index = lax.broadcasted_iota(jnp.int32, shape, dim)
    total = jnp.zeros(shape, jnp.int32)
    for slot in range(ends_ref.shape[0]):
        total = total + (index >= ends_ref[slot]).astype(jnp.int32)
    return index, total


def write_rows(core_ref, own_ref, other_ref, dest_ref):
    half = own_ref.shape[0]
    mine = pl.multiple_of(core_ref[0] * half, half)
    theirs = pl.multiple_of((1 - core_ref[0]) * half, half)
    dest_ref[pl.ds(mine, half), :] = own_ref[...]
    dest_ref[pl.ds(theirs, half), :] = other_ref[...]


def fetch(sources, buffers, sems):
    copies = [pltpu.make_async_copy(s, b, sems.at[i]) for i, (s, b) in enumerate(zip(sources, buffers))]
    for copy in copies:
        copy.start()
    return copies


def heads_forward(a, wq_ref, wk_ref, wv_ref, cos, sin, bias_ref, q_ref, k_ref, v_ref, o_ref, copies):
    for copy in copies:
        copy.wait()
    rows, width = q_ref.shape
    half = rows // 2
    wide = 256
    for tile in range(width // wide):
        span = slice(tile * wide, (tile + 1) * wide)
        ql = dot(a, wq_ref[:, span])
        kl = dot(a, wk_ref[:, span])
        vl = dot(a, wv_ref[:, span])
        for part in range(wide // PAIR):
            at = slice(part * PAIR, (part + 1) * PAIR)
            to = slice(tile * wide + part * PAIR, tile * wide + (part + 1) * PAIR)
            u = ql[:, at]
            q_ref[:, to] = (u * cos + partner_of(u) * sin).astype(BF16) * jnp.asarray(0.125, BF16)
            u = kl[:, at]
            k_ref[:, to] = (u * cos + partner_of(u) * sin).astype(BF16)
            v_ref[:, to] = vl[:, at].astype(BF16)
    for pair in range(width // PAIR):
        to = slice(pair * PAIR, (pair + 1) * PAIR)
        keys = k_ref[:, to]
        values = v_ref[:, to]
        masked = [(half_mask(keys, w), half_mask(values, w)) for w in range(2)]
        for block in range(2):
            at = slice(block * half, (block + 1) * half)
            reach = (block + 1) * half
            query = q_ref[at, to]
            total = jnp.zeros((half, PAIR), F32)
            for km, vm in masked:
                s = dot_t(query, km[:reach]) + bias_ref[at, :reach]
                s = jnp.exp(s - jnp.max(s, axis=-1, keepdims=True))
                p = (s * (1.0 / jnp.sum(s, axis=-1, keepdims=True))).astype(BF16)
                total = total + dot(p, vm[:reach])
            o_ref[at, to] = total.astype(BF16)


def fill_bias(ends_ref, bias_ref, keys_first):
    rows = bias_ref.shape[0]
    row_index, row_segment = segments(ends_ref, (rows, 1), 0)
    lane_index, lane_segment = segments(ends_ref, (1, rows), 1)
    if keys_first:
        allowed = (row_segment == lane_segment) & (row_index <= lane_index)
    else:
        allowed = (row_segment == lane_segment) & (lane_index <= row_index)
    bias_ref[...] = jnp.where(allowed, 0.0, NEGATIVE)


def first_heads(core, ends, own, other, gain, bias, cos, sin, wq, wk, wv, a_out, q, k, v, o,
                x_s, mask_s, wq_s, wk_s, wv_s, sems):
    copies = fetch((wq, wk, wv), (wq_s, wk_s, wv_s), sems)
    write_rows(core, own, other, x_s)
    unit, _ = norm_parts(x_s[...].astype(F32))
    a_out[...] = (unit * gain[...] + bias[...]).astype(BF16)
    fill_bias(ends, mask_s, False)
    heads_forward(a_out[...], wq_s, wk_s, wv_s, cos[...], sin[...], mask_s, q, k, v, o, copies)


def second_heads(
    core, ends, own, other, a, cos, sin, o_first,
    merge_gain, merge_bias, inlet_gain, inlet_bias, wq, wk, wv, wo_first, wo,
    q, k, v, o, z_out, h_out, c_out, x_s, mask_s, wq_s, wk_s, wv_s, first_s, wo_s, sems,
):
    copies = fetch((wq, wk, wv, wo_first, wo), (wq_s, wk_s, wv_s, first_s, wo_s), sems)
    write_rows(core, own, other, x_s)
    fill_bias(ends, mask_s, False)
    heads_forward(a[...], wq_s, wk_s, wv_s, cos[...], sin[...], mask_s, q, k, v, o, copies[:3])
    for copy in copies[3:]:
        copy.wait()
    z = dot(o_first[...], first_s[...]) + dot(o[...], wo_s[...])
    z_out[...] = z
    unit, _ = norm_parts(z)
    h = x_s[...].astype(F32) + (unit * merge_gain[...] + merge_bias[...])
    h_out[...] = h
    unit, _ = norm_parts(h)
    c_out[...] = (unit * inlet_gain[...] + inlet_bias[...]).astype(BF16)


def gelu_parts(f):
    x = jnp.abs(f) * 0.7071067811865476
    t = 1.0 / (1.0 + 0.3275911 * x)
    poly = t * (0.254829592 + t * (-0.284496736 + t * (1.421413741 + t * (-1.453152027 + t * 1.061405429))))
    bell = jnp.exp(-x * x)
    tail = 0.5 * poly * bell
    phi = jnp.where(f >= 0, 1.0 - tail, tail)
    return f * phi, phi + f * (0.3989422804014327 * bell)


def fetch_tiles(wi, wo, wi_s, wo_s, sems, first):
    count, _, tile = wi_s.shape
    copies = []
    for i in range(count):
        at = pl.ds((first + i) * tile, tile)
        copies.append(fetch((wi.at[:, at], wo.at[at, :]), (wi_s.at[i], wo_s.at[i]), sems.at[i]))
    return copies


def units_forward(c_ref, wi, wo, e_out, slope_out, wi_s, wo_s, sems):
    copies = fetch_tiles(wi, wo, wi_s, wo_s, sems, 0)
    count, _, tile = wi_s.shape
    c = c_ref[...]
    total = None
    before = None
    for i in range(count + 1):
        if i < count:
            for copy in copies[i]:
                copy.wait()
            f = dot(c, wi_s[i])
        if before is not None:
            part = dot(before, wo_s[i - 1])
            total = part if total is None else total + part
        if i < count:
            e, slope = gelu_parts(f)
            before = e.astype(BF16)
            e_out[:, i * tile:(i + 1) * tile] = before
            slope_out[i] = slope.astype(BF16)
    return total


def first_units(c, wi, wo, e_out, slope_out, n_out, wi_s, wo_s, sems):
    n_out[...] = units_forward(c, wi, wo, e_out, slope_out, wi_s, wo_s, sems)


def second_units(core, c, n_first, h, cot_own, cot_other, gain, bias, wi, wo,
                 e_out, slope_out, y_out, n_grad, gain_out, bias_out, y_s, wi_s, wo_s, sems):
    n = n_first[...] + units_forward(c, wi, wo, e_out, slope_out, wi_s, wo_s, sems)
    write_rows(core, cot_own, cot_other, y_s)
    unit, scale = norm_parts(n)
    y_out[...] = (h[...] + (unit * gain[...] + bias[...])).astype(BF16)
    below, gains, biases = norm_back(y_s[...].astype(F32), unit, scale, gain[...])
    n_grad[...] = below.astype(BF16)
    gain_out[...] = gains
    bias_out[...] = biases


def outer_terms(e, n_grad, out):
    out[...] = dot_rows(e[...], n_grad[...]).astype(BF16)


def units_back(first, n_grad, c, slope, wi, wo, inner_out, wi_s, wo_s, sems):
    copies = fetch_tiles(wi, wo, wi_s, wo_s, sems, first)
    count, _, tile = wi_s.shape
    total = None
    for i in range(count):
        for copy in copies[i]:
            copy.wait()
        f_grad = (dot_t(n_grad[...], wo_s[i]) * slope[first + i].astype(F32)).astype(BF16)
        inner_out[i] = dot_rows(c[...], f_grad).astype(BF16)
        part = dot_t(f_grad, wi_s[i])
        total = part if total is None else total + part
    return total


def first_units_back(first, n_grad, c, slope, wi, wo, inner_out, c_grad, wi_s, wo_s, sems):
    c_grad[...] = units_back(first, n_grad, c, slope, wi, wo, inner_out, wi_s, wo_s, sems)


def more_units_back(first, n_grad, c, slope, c_before, wi, wo, inner_out, c_grad, wi_s, wo_s, sems):
    c_grad[...] = c_before[...] + units_back(first, n_grad, c, slope, wi, wo, inner_out, wi_s, wo_s, sems)


def last_units_back(first, core, n_grad, c, slope, c_first, cot_own, cot_other, h, z, inlet_gain, merge_gain, wi, wo,
                    inner_out, h_grad, z_grad, sums_out, y_s, wi_s, wo_s, sems):
    c_grad = c_first[...] + units_back(first, n_grad, c, slope, wi, wo, inner_out, wi_s, wo_s, sems)
    write_rows(core, cot_own, cot_other, y_s)
    unit, scale = norm_parts(h[...])
    below, inlet_gains, inlet_biases = norm_back(c_grad, unit, scale, inlet_gain[...])
    h_part = y_s[...].astype(F32) + below
    h_grad[...] = h_part
    unit, scale = norm_parts(z[...])
    below, merge_gains, merge_biases = norm_back(h_part, unit, scale, merge_gain[...])
    z_grad[...] = below.astype(BF16)
    sums_out[0:1, :] = merge_gains
    sums_out[1:2, :] = merge_biases
    sums_out[2:3, :] = inlet_gains
    sums_out[3:4, :] = inlet_biases


def heads_back(ends, z_grad, a, cos, sin, q, k, v, o, weights,
               qk_out, vo_out, mask_s, ql_s, kl_s, vl_s, o_s, wq, wk, wv, wo, sems):
    copies = fetch(weights, (wo, wq, wk, wv), sems)
    rows, width = q.shape
    half = rows // 2
    fill_bias(ends, mask_s, True)
    copies[0].wait()
    o_s[...] = dot_t(z_grad[...], wo[...]).astype(BF16)
    for part in range(2):
        at = slice(part * width, (part + 1) * width)
        vo_out[1, at, :] = dot_rows(o[...], z_grad[:, at]).astype(BF16)
    cosine, sine = cos[...], sin[...]
    for pair in range(width // PAIR):
        to = slice(pair * PAIR, (pair + 1) * PAIR)
        query, keys, values, mixed = q[:, to], k[:, to], v[:, to], o_s[:, to]
        key_acc = [jnp.zeros((half, PAIR), F32) for _ in range(2)]
        value_acc = [jnp.zeros((half, PAIR), F32) for _ in range(2)]
        query_acc = [jnp.zeros((half, PAIR), F32) for _ in range(2)]
        for which in range(2):
            qm, km, vm, om = (half_mask(t, which) for t in (query, keys, values, mixed))
            for block in range(2):
                at = slice(block * half, (block + 1) * half)
                reach = (block + 1) * half
                s = dot_t(km[:reach], query[at]) + mask_s[:reach, at]
                s = jnp.exp(s - jnp.max(s, axis=0, keepdims=True))
                p = s * (1.0 / jnp.sum(s, axis=0, keepdims=True))
                grown = dot_t(vm[:reach], mixed[at])
                offset = jnp.sum(p * grown, axis=0, keepdims=True)
                ds = (p * (grown - offset)).astype(BF16)
                p = p.astype(BF16)
                query_acc[block] = query_acc[block] + dot_rows(ds, km[:reach])
                for piece in range(block + 1):
                    rs = slice(piece * half, (piece + 1) * half)
                    key_acc[piece] = key_acc[piece] + dot(ds[rs], qm[at])
                    value_acc[piece] = value_acc[piece] + dot(p[rs], om[at])
        for block in range(2):
            at = slice(block * half, (block + 1) * half)
            u = query_acc[block] * 0.125
            ql_s[at, to] = (u * cosine[at] - partner_of(u) * sine[at]).astype(BF16)
            u = key_acc[block]
            kl_s[at, to] = (u * cosine[at] - partner_of(u) * sine[at]).astype(BF16)
            vl_s[at, to] = value_acc[block].astype(BF16)
    a_all = a[...]
    qk_out[0] = dot_rows(a_all, ql_s[...]).astype(BF16)
    qk_out[1] = dot_rows(a_all, kl_s[...]).astype(BF16)
    vo_out[0] = dot_rows(a_all, vl_s[...]).astype(BF16)
    for copy in copies[1:]:
        copy.wait()
    return dot_t(ql_s[...], wq[...]) + dot_t(kl_s[...], wk[...]) + dot_t(vl_s[...], wv[...])


def first_heads_back(ends, z_grad, a, cos, sin, q, k, v, o, wo, wq, wk, wv, qk_out, vo_out, a_grad, *scratch):
    a_grad[...] = heads_back(ends, z_grad, a, cos, sin, q, k, v, o, (wo, wq, wk, wv), qk_out, vo_out, *scratch)


def second_heads_back(core, ends, z_grad, a, cos, sin, q, k, v, o, a_first, own, other, h_grad, gain, wo, wq, wk, wv,
                      qk_out, vo_out, x_grad, gain_out, bias_out, x_s, *scratch):
    a_grad = a_first[...] + heads_back(
        ends, z_grad, a, cos, sin, q, k, v, o, (wo, wq, wk, wv), qk_out, vo_out, *scratch)
    write_rows(core, own, other, x_s)
    unit, scale = norm_parts(x_s[...].astype(F32))
    below, gains, biases = norm_back(a_grad, unit, scale, gain[...])
    x_grad[...] = (h_grad[...] + below).astype(BF16)
    gain_out[...] = gains
    bias_out[...] = biases


SMEM = pl.BlockSpec(memory_space=pltpu.SMEM)
FULL = pl.BlockSpec(memory_space=pltpu.VMEM)
FAR = pl.BlockSpec(memory_space=pltpu.HBM)


def params(limit, **kw):
    return pltpu.CompilerParams(vmem_limit_bytes=limit * 2**20, **kw)


def shape(dims, kind=BF16):
    return jax.ShapeDtypeStruct(dims, kind)


def call(kernel, operands, outs, scratch, smem, limit, far=0):
    specs = [SMEM] * smem + [FULL] * (len(operands) - smem - far) + [FAR] * far
    return pl.pallas_call(
        kernel,
        in_specs=specs,
        out_specs=[FULL] * len(outs),
        out_shape=outs,
        scratch_shapes=scratch,
        compiler_params=params(limit),
        cost_estimate=pl.CostEstimate(flops=COST, bytes_accessed=2**20, transcendentals=0),
    )(*operands)


def tiled(kernel, operands, kinds, outs, out_kinds, scratch, tile, steps, limit, first=0):
    def spec(kind, dims, first=0):
        if kind == "s":
            return SMEM
        if kind == "f":
            return pl.BlockSpec(dims, lambda i: (0,) * len(dims))
        if kind == "3":
            return pl.BlockSpec((1, *dims[1:]), lambda i: (i, 0, 0))
        if kind == "c":
            return pl.BlockSpec((dims[0], tile), lambda i: (0, i + first))
        return pl.BlockSpec((tile, dims[1]), lambda i: (i + first, 0))
    return pl.pallas_call(
        kernel,
        grid=(steps,),
        in_specs=[spec(kind, op.shape, first) for kind, op in zip(kinds, operands)],
        out_specs=[spec(kind, out.shape) for kind, out in zip(out_kinds, outs)],
        out_shape=outs,
        scratch_shapes=scratch,
        compiler_params=params(limit, dimension_semantics=("arbitrary",)),
        cost_estimate=pl.CostEstimate(flops=COST, bytes_accessed=2**20, transcendentals=0),
    )(*operands)


def swap(value):
    return lax.ppermute(value, "tensor", SWAP)


def coordinates(mesh):
    total = mesh.shape["dp"]
    places = [getattr(d, "coords", None) for d in mesh.devices.reshape(total, -1)[:, 0]]
    if all(p is not None and len(p) == 3 for p in places):
        sizes = [len({p[i] for p in places}) for i in range(3)]
        low = [min(p[i] for p in places) for i in range(3)]
        order = [((p[2] - low[2]) * sizes[1] + p[1] - low[1]) * sizes[0] + p[0] - low[0] for p in places]
        if order == list(range(total)):
            return tuple(sizes)
    return (2, 2, total // 4) if total % 4 == 0 else (1, 1, total)


def add(*terms):
    total = terms[0].astype(F32)
    for term in terms[1:]:
        total = total + term.astype(F32)
    return total.astype(BF16)


class Line:
    def __init__(self, token):
        self.token = token

    def fence(self, values):
        self.token, values = lax.optimization_barrier((self.token, values))
        return values

    def done(self, value):
        self.token = value
        return value


def settle_kernel(count, spots, *refs):
    *pieces, out = refs
    pieces = pieces[-4:]
    step = pl.program_id(0)
    size = pieces[0].shape[0]
    per = 4 // count
    for i, piece in enumerate(pieces):
        if count == 1:
            out[pl.ds(pl.multiple_of(spots[i] * size, size), size), :] = piece[...].astype(F32)
        else:
            @pl.when(spots[i] // per == step)
            def _():
                at = spots[i] % per
                out[pl.ds(pl.multiple_of(at * size, size), size), :] = piece[...].astype(F32)


def settle(spots, pieces, whole, dims, blocks, count):
    lines, columns = 4 * pieces[0].shape[0] // count, pieces[0].shape[1]
    before = [] if whole is None else [whole]
    base, last = blocks[0], blocks[-1]
    return pl.pallas_call(
        functools.partial(settle_kernel, count),
        grid=(count,),
        in_specs=[SMEM] + [pl.BlockSpec(memory_space=pl.ANY)] * len(before)
        + [pl.BlockSpec(p.shape, lambda i: (0, 0)) for p in pieces],
        out_specs=pl.BlockSpec((lines, columns), lambda i: (base[0], base[1] + i)),
        out_shape=shape(dims, F32),
        input_output_aliases={1: 0} if before else {},
        compiler_params=pltpu.CompilerParams(vmem_limit_bytes=20 * 2**20),
        cost_estimate=pl.CostEstimate(flops=COST, bytes_accessed=2**20, transcendentals=0),
    )(spots, *before, *pieces)


def settle_heads_kernel(folded, spots, *refs):
    pieces, (top, bottom) = refs[:4], refs[4:]
    size = pieces[0].shape[0]
    for i, piece in enumerate(pieces):
        for spot in range(4):
            @pl.when(spots[i] == spot)
            def _():
                at = spot % 2
                if spot < 2:
                    top[at * size:(at + 1) * size, :] = piece[...].astype(F32)
                elif folded:
                    bottom[:, at * size:(at + 1) * size] = piece[...].astype(F32)
                else:
                    bottom[at * size:(at + 1) * size, :] = piece[...].astype(F32)


def settle_heads(spots, pieces, folded):
    lines, columns = pieces[0].shape
    return pl.pallas_call(
        functools.partial(settle_heads_kernel, folded),
        in_specs=[SMEM] + [FULL] * 4,
        out_specs=[FULL, FULL],
        out_shape=[shape((2 * lines, columns), F32), shape((lines, 2 * columns) if folded else (2 * lines, columns), F32)],
        compiler_params=pltpu.CompilerParams(vmem_limit_bytes=12 * 2**20),
        cost_estimate=pl.CostEstimate(flops=COST, bytes_accessed=2**20, transcendentals=0),
    )(spots, *pieces)


class Chunk:
    def __init__(self, line, here, core, peer, finish):
        self.line, self.finish = line, finish
        self.own, self.other = None, swap(peer)
        self.a, self.z, self.b = jnp.where(core == 0, here[1], here[2]), here[4], jnp.where(core == 0, here[2], here[1])

    def part(self, value, *picks):
        value = value.reshape(*([2] * len(picks)), -1, value.shape[-1])
        for p in picks:
            value = lax.dynamic_index_in_dim(value, p, 0, keepdims=False)
        return value

    def trade(self, value, *bits):
        pairs = [(2 * i + c, 2 * (i ^ bits[c]) + c) for i in range(lax.axis_size("dp")) for c in range(2)]
        return lax.ppermute(value, ("dp", "tensor"), pairs)

    LANDS = {"c": "other", "a": "first", "b": "second", "d": "third", "e": "fourth", "f": "fifth",
             "g": "sixth", "h": "near", "k": "far"}

    def step(self, what):
        if what in self.LANDS:
            self.land(self.LANDS[what])
        else:
            getattr(self, "step" + what)()

    def land(self, name):
        setattr(self, name, self.line.fence(getattr(self, name)))

    def step0(self):
        own, other = self.line.fence((self.own, self.other))
        send = self.line.done(add(self.part(own, 1 - self.a), self.part(other, 1 - self.a)))
        self.first = self.trade(send, 1, 2)

    def step1(self):
        own, other, first = self.line.fence((self.own, self.other, self.first))
        a, z = self.a, 1 - self.z
        send = self.line.done(add(self.part(own, a, z), self.part(other, a, z), self.part(first, z)))
        self.second = self.trade(send, 4, 4)

    def step2(self):
        own, other, first, second = self.line.fence((self.own, self.other, self.first, self.second))
        a, z, b = self.a, self.z, 1 - self.b
        send = self.line.done(add(self.part(own, a, z, b), self.part(other, a, z, b), self.part(first, z, b), self.part(second, b)))
        self.third = self.trade(send, 2, 1)

    def step3(self):
        own, other, first, second, third = self.line.fence((self.own, self.other, self.first, self.second, self.third))
        a, z, b = self.a, self.z, self.b
        self.kept = self.line.done(add(self.part(own, a, z, b), self.part(other, a, z, b), self.part(first, z, b),
                                       self.part(second, b), third))
        self.fourth = self.trade(self.kept, 8, 8)

    def step4(self):
        kept, fourth = self.line.fence((self.kept, self.fourth))
        self.total = self.line.done(add(kept, fourth))
        self.fifth = self.trade(self.total, 2, 1)

    def step5(self):
        total, fifth = self.line.fence((self.total, self.fifth))
        low = self.b == 0
        self.mine = self.line.done(jnp.concatenate([jnp.where(low, total, fifth), jnp.where(low, fifth, total)], axis=0))
        self.sixth = self.trade(self.mine, 4, 4)
        self.near = self.trade(self.mine, 1, 2)

    def step6(self):
        self.sixth = self.line.done(self.line.fence(self.sixth))
        self.far = self.trade(self.sixth, 1, 2)

    def step7(self):
        pieces = self.line.fence((self.mine, self.sixth, self.near, self.far))
        a, z = self.a, self.z
        spots = jnp.stack([2 * a + z, 2 * a + 1 - z, 2 * (1 - a) + z, 2 * (1 - a) + 1 - z])
        self.line.done(self.finish(spots, pieces))


class Norms(Chunk):
    def __init__(self, line, values):
        self.line, self.values = line, values
        self.bits = (None, 1, 2, 4, 8)

    def step(self, what):
        if not what.isdigit():
            return self.land("other")
        number = int(what)
        if number == 0:
            self.values = self.line.fence(self.values)
        else:
            values, other = self.line.fence((self.values, self.other))
            self.values = self.line.done(values + other)
        if number < len(self.bits):
            bit = self.bits[number]
            self.other = swap(self.values) if bit is None else self.trade(self.values, bit, bit)


class Spread(Chunk):
    def __init__(self, line, core, full):
        self.line, self.core = line, core
        self.parts = full.reshape(2, full.shape[0] // 2, full.shape[1])

    def step(self, what):
        if what == "0":
            parts = self.line.fence(self.parts)
            self.mine = lax.dynamic_index_in_dim(parts, self.core, 0, keepdims=False)
            self.other = swap(self.line.done(lax.dynamic_index_in_dim(parts, 1 - self.core, 0, keepdims=False)))
        elif what == "1":
            mine, other = self.line.fence((self.mine, self.other))
            first = self.core == 0
            self.result = self.line.done(jnp.stack([jnp.where(first, mine, other), jnp.where(first, other, mine)]))
        else:
            self.land("other")


ORDER = (
    "G00", "G01", "y00", "G10", "G11", "o0c", "y0c", "y01", "o00", "o1c", "o10", "K00", "K01", "K10", "o0a", "i0c",
    "i00", "o01", "i1c", "K11", "o1a", "i10", "o11", "i0a", "i01", "o0b", "o02", "i1a", "H0", "o1b", "i0b", "o0d",
    "i02", "i11", "h0c", "o12", "i0d", "i03", "h1c", "o03", "o1d", "o13", "H1", "i1b", "i0e", "i04", "h00", "o0e",
    "h10", "o1e", "i0f", "i05", "i12", "h0a", "x00", "x0c", "h01", "i0g", "i06", "x01", "h1a", "o14", "i0h", "h11",
    "i1d", "i13", "h0b", "h02", "i0k", "i07", "o1f", "o15", "h0d", "h03", "h1b", "h12", "o1h", "n00", "n0a", "o04",
    "h1d", "h13", "i1e", "i14", "o0f", "n01", "o1g", "o16", "i1f", "n0b", "o05", "o1k", "h0e", "i15", "h1e", "h04",
    "o0h", "h14", "o17", "o0g", "i1h", "n02", "o06", "h0f", "h1f", "h05", "n0d", "i1g", "h15", "o0k", "i16", "h0h",
    "n03", "o07", "h0g", "h06", "h1h", "i1k", "i17", "h1g", "h16", "n0e", "h0k", "h07", "n04", "n0f", "n05", "h1k",
    "h17",
)

LIMITS = {'a1': 10, 'a2': 13, 'u1': 15, 'u2': 20, 'g': 9, 'k': 12, 'l': 15, 'h1': 19, 'h2': 19}


def on_device(
    sizes, inputs, lengths, query_weight, key_weight, value_weight, output_weight, inner_weight, outer_weight,
    entry_gain, entry_bias, merge_gain, merge_bias, inlet_gain, inlet_bias, outlet_gain, outlet_bias, cotangent,
):
    core = lax.axis_index("tensor").astype(jnp.int32)
    core_s = core.reshape(1)
    half = inputs.shape[1]
    rows = 2 * half
    width = query_weight.shape[1]
    units = inner_weight.shape[1]
    feats = inputs.shape[2]
    row = lambda v: v.reshape(1, feats)
    pick = lambda v, i: lax.dynamic_index_in_dim(v, i, 0, keepdims=False)
    x_own = pick(inputs, core)
    x_other = swap(pick(inputs, 1 - core))
    wq2, wk2, wv2 = swap(query_weight), swap(key_weight), swap(value_weight)
    wo2, wi2, wf2 = swap(output_weight), swap(inner_weight), swap(outer_weight)
    y_own = pick(cotangent, core)
    y_other = swap(pick(cotangent, 1 - core))

    lens = pick(lengths, core)[0]
    slot = jnp.arange(lens.shape[0], dtype=jnp.int32)
    ends = jnp.sum(jnp.where(slot[None, :] <= slot[:, None], lens[None, :], 0), axis=1)
    index = jnp.arange(rows, dtype=jnp.int32)
    begin = jnp.max(jnp.where(index[:, None] >= ends[None, :], ends[None, :], 0), axis=1)
    place = (index - begin).astype(F32)
    lane = jnp.arange(PAIR, dtype=jnp.int32)
    rate = jnp.exp((lane % (HEAD // 2)).astype(F32) * (-math.log(10000.0) / (HEAD // 2)))
    angle = place[:, None] * rate[None, :]
    cos = jnp.cos(angle)
    sin = jnp.sin(angle) * jnp.where(lane % HEAD < HEAD // 2, -1.0, 1.0)[None, :]

    act = shape((rows, width))
    mask = pltpu.VMEM((rows, rows), F32)
    xbuf = pltpu.VMEM((rows, feats), BF16)
    vmem = lambda dims, kind=BF16: pltpu.VMEM(dims, kind)
    dma = lambda *dims: pltpu.SemaphoreType.DMA(dims)
    head_bufs = [vmem((feats, width))] * 3
    a, q1, k1, v1, o1 = call(
        first_heads,
        [core_s, ends, x_own, x_other, row(entry_gain), row(entry_bias), cos, sin, query_weight, key_weight, value_weight],
        [shape((rows, feats)), act, act, act, act], [xbuf, mask, *head_bufs, dma(3)], 2, LIMITS["a1"], 3)
    q2, k2, v2, o2, z, h, c = call(
        second_heads,
        [core_s, ends, x_own, x_other, a, cos, sin, o1,
         row(merge_gain), row(merge_bias), row(inlet_gain), row(inlet_bias), wq2, wk2, wv2, output_weight, wo2],
        [act, act, act, act, shape((rows, feats), F32), shape((rows, feats), F32), shape((rows, feats))],
        [xbuf, mask, *head_bufs, vmem((width, feats)), vmem((width, feats)), dma(5)], 2, LIMITS["a2"], 5)
    tile = 512
    steps = units // tile
    big = shape((rows, units))
    steep = shape((steps, rows, tile))
    unit_bufs = lambda n: [vmem((n, feats, tile)), vmem((n, tile, feats)), dma(n, 2)]
    e1, s1, n1 = call(first_units, [c, inner_weight, outer_weight],
                      [big, steep, shape((rows, feats), F32)], unit_bufs(steps), 0, LIMITS["u1"], 2)
    e2, s2, y, n_grad, outlet_gains, outlet_biases = call(
        second_units, [core_s, c, n1, h, y_own, y_other, row(outlet_gain), row(outlet_bias), wi2, wf2],
        [big, steep, shape((rows, feats)), shape((rows, feats)), shape((1, feats), F32), shape((1, feats), F32)],
        [xbuf, *unit_bufs(steps)], 1, LIMITS["u2"], 2)
    total = shape((rows, feats), F32)
    line = Line(n_grad)
    made = {"c": None}
    wholes = {}
    scratch = [mask] + [vmem((rows, width))] * 4 + head_bufs + [vmem((width, feats)), dma(4)]
    grads = [shape((2, feats, width)), shape((2, feats, width))]

    def outer_step(pair, mine):
        e_in, n_in = line.fence(((e2, e1)[mine], n_grad))
        (out,) = tiled(outer_terms, [e_in, n_in], "cf", [shape((2 * tile, feats))], "r", [], 2 * tile, 1, LIMITS["g"], pair)
        line.done(out)
        return [out]

    def inner_step(pair, mine):
        ng, cc, slope, wi, wo = line.fence([n_grad, c, *((s2, wi2, wf2), (s1, inner_weight, outer_weight))[mine]])
        outs = [shape((2, feats, tile)), total]
        bufs = unit_bufs(2)
        with_first = lambda kernel: functools.partial(kernel, 2 * pair)
        if made["c"] is None:
            out, made["c"] = call(with_first(first_units_back), [ng, cc, slope, wi, wo], outs, bufs, 0, LIMITS["k"], 2)
        elif pair == steps // 2 - 1 and mine:
            out, made["h"], made["z"], made["sums"] = call(
                with_first(last_units_back),
                [core_s, ng, cc, slope, made["c"], y_own, y_other, h, z, row(inlet_gain), row(merge_gain), wi, wo],
                [outs[0], total, shape((rows, feats)), shape((4, feats), F32)], [xbuf, *bufs], 1, LIMITS["l"], 2)
        else:
            out, made["c"] = call(with_first(more_units_back), [ng, cc, slope, made["c"], wi, wo], outs, bufs, 0, LIMITS["k"], 2)
        line.done(out)
        return [out.reshape(2 * feats, tile)]

    def heads_step(mine):
        z_grad = line.fence(made["z"])
        if not mine:
            qk, vo, made["a"] = call(
                first_heads_back, [ends, z_grad, a, cos, sin, q2, k2, v2, o2, wo2, wq2, wk2, wv2],
                grads + [total], scratch, 1, LIMITS["h1"], 4)
        else:
            qk, vo, made["x"], made["gain"], made["bias"] = call(
                second_heads_back,
                [core_s, ends, z_grad, a, cos, sin, q1, k1, v1, o1, made["a"], x_own, x_other, made["h"], row(entry_gain),
                 output_weight, query_weight, key_weight, value_weight],
                grads + [shape((rows, feats)), shape((1, feats), F32), shape((1, feats), F32)], [xbuf] + scratch, 2,
                LIMITS["h2"], 4)
        line.done(qk)
        return [qk.reshape(2 * feats, width), vo.reshape(2 * feats, width)]

    place_of = lax.axis_index("dp").astype(jnp.int32)
    here = {bit: (place_of // bit) % 2 for bit in (1, 2, 4, 8)}
    outs = {"o": (units, feats), "i": (feats, units)}

    def finisher(name):
        kind, number = name[0], int(name[1])

        def finish(spots, pieces):
            if kind == "o":
                wholes["o"] = settle(spots, pieces, wholes.get("o"), outs["o"], [(number, 0)], 1)
                return wholes["o"]
            if kind == "i":
                wholes["i"] = settle(spots, pieces, wholes.get("i"), outs["i"], [(0, 2 * number), (0, 2 * number + 1)], 2)
                return wholes["i"]
            wholes[name] = settle_heads(spots, pieces, number == 1)
            return wholes[name][1]
        return finish

    chunks = {"y0": Spread(line, core, y)}
    fast = tuple(sizes) == (2, 2, 4)
    plain = {}

    def peers(name, peer):
        if fast:
            chunks[name] = Chunk(line, here, core, peer, finisher(name))
        else:
            plain[name] = peer

    def owns(name, own):
        if fast:
            chunks[name].own = own
        else:
            wholes[name] = lax.psum(add(own, swap(plain[name])), "dp").astype(F32)

    for what in ORDER:
        name, last = what[:-1], what[-1]
        if name[0] in "GK":
            which, mine = int(name[1]), int(last)
            (made_now,) = (outer_step if name[0] == "G" else inner_step)(which, mine)
            (peers, owns)[mine](("o" if name[0] == "G" else "i") + str(which), made_now)
        elif name == "H":
            mine = int(last)
            for i, made_now in enumerate(heads_step(mine)):
                (peers, owns)[mine]("h" + str(i), made_now)
            if mine:
                sums = made["sums"]
                norms = [made["gain"], made["bias"], sums[0:1], sums[1:2], sums[2:3], sums[3:4], outlet_gains, outlet_biases]
                chunks["n0"] = Norms(line, jnp.concatenate(norms, axis=0))
                chunks["x0"] = Spread(line, core, made["x"])
        elif fast or name in ("x0", "y0"):
            chunks[name].step(last)
    outputs, input_grad = chunks["y0"].result, chunks["x0"].result
    norms = chunks["n0"].values
    if not fast:
        norms = lax.psum(norms, ("dp", "tensor"))
    if not fast:
        wholes["o"] = jnp.concatenate([wholes["o" + str(i)] for i in range(steps // 2)], axis=0)
        wholes["i"] = jnp.concatenate(
            [half for i in range(steps // 2) for half in jnp.split(wholes["i" + str(i)], 2, axis=0)], axis=1)
        wholes["h0"] = jnp.split(wholes["h0"], 2, axis=0)
        value, folded = jnp.split(wholes["h1"], 2, axis=0)
        wholes["h1"] = [value, jnp.concatenate([folded[:width], folded[width:]], axis=1)]
    query_grad, key_grad = wholes["h0"]
    value_grad, output_grad = wholes["h1"]
    inner_grad, outer_grad = wholes["i"], wholes["o"]
    weight_grads = [query_grad, key_grad, value_grad, output_grad, inner_grad, outer_grad]
    return (outputs, input_grad, *weight_grads, *[norms[i] for i in range(8)])


def solution(mesh):
    rows = P(None, ("dp", "tensor"), None)
    columns, lines = P(None, "tensor"), P("tensor", None)
    weights = (columns, columns, columns, lines, columns, lines)
    return jax.shard_map(
        functools.partial(on_device, coordinates(mesh)),
        mesh=mesh,
        in_specs=(rows, P(None, "dp", None), *weights, *([P()] * 8), rows),
        out_specs=(rows, rows, *weights, *([P()] * 8)),
        check_vma=False,
    )
```

```python
import functools
import math

import jax
import jax.numpy as jnp
from jax import lax
from jax.experimental import pallas as pl
from jax.experimental.pallas import tpu as pltpu
from jax.sharding import PartitionSpec as P

HEAD = 64
PAIR = 128
COST = 2 * 10**10
NEGATIVE = -1e30
F32 = jnp.float32
BF16 = jnp.bfloat16
SWAP = [(0, 1), (1, 0)]


def dot(left, right):
    return jnp.dot(left, right, preferred_element_type=F32)


def dot_rows(left, right):
    return lax.dot_general(left, right, (((0,), (0,)), ((), ())), preferred_element_type=F32)


def dot_t(left, right):
    return lax.dot_general(left, right, (((1,), (1,)), ((), ())), preferred_element_type=F32)


def norm_parts(values):
    center = values - jnp.mean(values, axis=-1, keepdims=True)
    scale = lax.rsqrt(jnp.mean(center * center, axis=-1, keepdims=True) + 1e-05)
    return center * scale, scale


def norm_back(grads, unit, scale, gain):
    inner = grads * gain
    first = jnp.mean(inner, axis=-1, keepdims=True)
    second = jnp.mean(inner * unit, axis=-1, keepdims=True)
    below = scale * (inner - first - unit * second)
    return (
        below,
        jnp.sum(grads * unit, axis=0, keepdims=True),
        jnp.sum(grads, axis=0, keepdims=True),
    )


def partner_of(values):
    lane = lax.broadcasted_iota(jnp.int32, values.shape, 1)
    return jnp.where((lane & 63) < 32, pltpu.roll(values, 96, 1), pltpu.roll(values, 32, 1))


def half_mask(values, which):
    lane = lax.broadcasted_iota(jnp.int32, values.shape, 1)
    keep = (lane < HEAD) if which == 0 else (lane >= HEAD)
    return jnp.where(keep, values, jnp.zeros_like(values))


def segments(ends_ref, shape, dim):
    index = lax.broadcasted_iota(jnp.int32, shape, dim)
    total = jnp.zeros(shape, jnp.int32)
    for slot in range(ends_ref.shape[0]):
        total = total + (index >= ends_ref[slot]).astype(jnp.int32)
    return index, total


def write_rows(core_ref, own_ref, other_ref, dest_ref):
    half = own_ref.shape[0]
    mine = pl.multiple_of(core_ref[0] * half, half)
    theirs = pl.multiple_of((1 - core_ref[0]) * half, half)
    dest_ref[pl.ds(mine, half), :] = own_ref[...]
    dest_ref[pl.ds(theirs, half), :] = other_ref[...]


def fetch(sources, buffers, sems):
    copies = [pltpu.make_async_copy(s, b, sems.at[i]) for i, (s, b) in enumerate(zip(sources, buffers))]
    for copy in copies:
        copy.start()
    return copies


def heads_forward(a, wq_ref, wk_ref, wv_ref, cos, sin, bias_ref, q_ref, k_ref, v_ref, o_ref):
    rows, width = q_ref.shape
    half = rows // 2
    wide = 256
    for tile in range(width // wide):
        span = slice(tile * wide, (tile + 1) * wide)
        ql = dot(a, wq_ref[:, span])
        kl = dot(a, wk_ref[:, span])
        vl = dot(a, wv_ref[:, span])
        for part in range(wide // PAIR):
            at = slice(part * PAIR, (part + 1) * PAIR)
            to = slice(tile * wide + part * PAIR, tile * wide + (part + 1) * PAIR)
            u = ql[:, at]
            q_ref[:, to] = (u * cos + partner_of(u) * sin).astype(BF16) * jnp.asarray(0.125, BF16)
            u = kl[:, at]
            k_ref[:, to] = (u * cos + partner_of(u) * sin).astype(BF16)
            v_ref[:, to] = vl[:, at].astype(BF16)
    for pair in range(width // PAIR):
        to = slice(pair * PAIR, (pair + 1) * PAIR)
        keys = k_ref[:, to]
        values = v_ref[:, to]
        masked = [(half_mask(keys, w), half_mask(values, w)) for w in range(2)]
        for block in range(2):
            at = slice(block * half, (block + 1) * half)
            reach = (block + 1) * half
            query = q_ref[at, to]
            total = jnp.zeros((half, PAIR), F32)
            for km, vm in masked:
                s = dot_t(query, km[:reach]) + bias_ref[at, :reach]
                s = jnp.exp(s - jnp.max(s, axis=-1, keepdims=True))
                p = (s * (1.0 / jnp.sum(s, axis=-1, keepdims=True))).astype(BF16)
                total = total + dot(p, vm[:reach])
            o_ref[at, to] = total.astype(BF16)


def fill_bias(ends_ref, bias_ref, keys_first):
    rows = bias_ref.shape[0]
    row_index, row_segment = segments(ends_ref, (rows, 1), 0)
    lane_index, lane_segment = segments(ends_ref, (1, rows), 1)
    if keys_first:
        allowed = (row_segment == lane_segment) & (row_index <= lane_index)
    else:
        allowed = (row_segment == lane_segment) & (lane_index <= row_index)
    bias_ref[...] = jnp.where(allowed, 0.0, NEGATIVE)


def first_heads(core, ends, own, other, gain, bias, cos, sin, wq, wk, wv, a_out, q, k, v, o,
                x_s, mask_s):
    write_rows(core, own, other, x_s)
    unit, _ = norm_parts(x_s[...].astype(F32))
    a_out[...] = (unit * gain[...] + bias[...]).astype(BF16)
    fill_bias(ends, mask_s, False)
    heads_forward(a_out[...], wq, wk, wv, cos[...], sin[...], mask_s, q, k, v, o)


def second_heads(
    core, ends, own, other, a, cos, sin, o_first,
    merge_gain, merge_bias, inlet_gain, inlet_bias, wq, wk, wv, wo_first, wo,
    q, k, v, o, z_out, h_out, c_out, x_s, mask_s,
):
    write_rows(core, own, other, x_s)
    fill_bias(ends, mask_s, False)
    heads_forward(a[...], wq, wk, wv, cos[...], sin[...], mask_s, q, k, v, o)
    z = dot(o_first[...], wo_first[...]) + dot(o[...], wo[...])
    z_out[...] = z
    unit, _ = norm_parts(z)
    h = x_s[...].astype(F32) + (unit * merge_gain[...] + merge_bias[...])
    h_out[...] = h
    unit, _ = norm_parts(h)
    c_out[...] = (unit * inlet_gain[...] + inlet_bias[...]).astype(BF16)


def gelu_parts(f):
    x = jnp.abs(f) * 0.7071067811865476
    t = 1.0 / (1.0 + 0.3275911 * x)
    poly = t * (0.254829592 + t * (-0.284496736 + t * (1.421413741 + t * (-1.453152027 + t * 1.061405429))))
    bell = jnp.exp(-x * x)
    tail = 0.5 * poly * bell
    phi = jnp.where(f >= 0, 1.0 - tail, tail)
    return f * phi, phi + f * (0.3989422804014327 * bell)


def fetch_tiles(wi, wo, wi_s, wo_s, sems, first):
    count, _, tile = wi_s.shape
    copies = []
    for i in range(count):
        at = pl.ds((first + i) * tile, tile)
        copies.append(fetch((wi.at[:, at], wo.at[at, :]), (wi_s.at[i], wo_s.at[i]), sems.at[i]))
    return copies


def units_forward(c_ref, wi, wo, e_out, slope_out, wi_s, wo_s, sems):
    copies = fetch_tiles(wi, wo, wi_s, wo_s, sems, 0)
    count, _, tile = wi_s.shape
    c = c_ref[...]
    total = None
    before = None
    for i in range(count + 1):
        if i < count:
            for copy in copies[i]:
                copy.wait()
            f = dot(c, wi_s[i])
        if before is not None:
            part = dot(before, wo_s[i - 1])
            total = part if total is None else total + part
        if i < count:
            e, slope = gelu_parts(f)
            before = e.astype(BF16)
            e_out[:, i * tile:(i + 1) * tile] = before
            slope_out[i] = slope.astype(BF16)
    return total


def first_units(c, wi, wo, e_out, slope_out, n_out, wi_s, wo_s, sems):
    n_out[...] = units_forward(c, wi, wo, e_out, slope_out, wi_s, wo_s, sems)


def second_units(core, c, n_first, h, cot_own, cot_other, gain, bias, wi, wo,
                 e_out, slope_out, y_out, n_grad, gain_out, bias_out, y_s, wi_s, wo_s, sems):
    n = n_first[...] + units_forward(c, wi, wo, e_out, slope_out, wi_s, wo_s, sems)
    write_rows(core, cot_own, cot_other, y_s)
    unit, scale = norm_parts(n)
    y_out[...] = (h[...] + (unit * gain[...] + bias[...])).astype(BF16)
    below, gains, biases = norm_back(y_s[...].astype(F32), unit, scale, gain[...])
    n_grad[...] = below.astype(BF16)
    gain_out[...] = gains
    bias_out[...] = biases


def outer_terms(e, n_grad, out):
    out[...] = dot_rows(e[...], n_grad[...]).astype(BF16)


def units_back(first, n_grad, c, slope, wi, wo, inner_out, wi_s, wo_s, sems):
    copies = fetch_tiles(wi, wo, wi_s, wo_s, sems, first)
    count, _, tile = wi_s.shape
    total = None
    for i in range(count):
        for copy in copies[i]:
            copy.wait()
        f_grad = (dot_t(n_grad[...], wo_s[i]) * slope[first + i].astype(F32)).astype(BF16)
        inner_out[i] = dot_rows(c[...], f_grad).astype(BF16)
        part = dot_t(f_grad, wi_s[i])
        total = part if total is None else total + part
    return total


def first_units_back(first, n_grad, c, slope, wi, wo, inner_out, c_grad, wi_s, wo_s, sems):
    c_grad[...] = units_back(first, n_grad, c, slope, wi, wo, inner_out, wi_s, wo_s, sems)


def more_units_back(first, n_grad, c, slope, c_before, wi, wo, inner_out, c_grad, wi_s, wo_s, sems):
    c_grad[...] = c_before[...] + units_back(first, n_grad, c, slope, wi, wo, inner_out, wi_s, wo_s, sems)


def last_units_back(first, core, n_grad, c, slope, c_first, cot_own, cot_other, h, z, inlet_gain, merge_gain, wi, wo,
                    inner_out, h_grad, z_grad, sums_out, y_s, wi_s, wo_s, sems):
    c_grad = c_first[...] + units_back(first, n_grad, c, slope, wi, wo, inner_out, wi_s, wo_s, sems)
    write_rows(core, cot_own, cot_other, y_s)
    unit, scale = norm_parts(h[...])
    below, inlet_gains, inlet_biases = norm_back(c_grad, unit, scale, inlet_gain[...])
    h_part = y_s[...].astype(F32) + below
    h_grad[...] = h_part
    unit, scale = norm_parts(z[...])
    below, merge_gains, merge_biases = norm_back(h_part, unit, scale, merge_gain[...])
    z_grad[...] = below.astype(BF16)
    sums_out[0:1, :] = merge_gains
    sums_out[1:2, :] = merge_biases
    sums_out[2:3, :] = inlet_gains
    sums_out[3:4, :] = inlet_biases


def heads_back(ends, z_grad, a, cos, sin, q, k, v, o, weights,
               qk_out, vo_out, mask_s, ql_s, kl_s, vl_s, o_s):
    wo, wq, wk, wv = weights
    rows, width = q.shape
    half = rows // 2
    fill_bias(ends, mask_s, True)
    o_s[...] = dot_t(z_grad[...], wo[...]).astype(BF16)
    for part in range(2):
        at = slice(part * width, (part + 1) * width)
        vo_out[1, at, :] = dot_rows(o[...], z_grad[:, at]).astype(BF16)
    cosine, sine = cos[...], sin[...]
    for pair in range(width // PAIR):
        to = slice(pair * PAIR, (pair + 1) * PAIR)
        query, keys, values, mixed = q[:, to], k[:, to], v[:, to], o_s[:, to]
        key_acc = [jnp.zeros((half, PAIR), F32) for _ in range(2)]
        value_acc = [jnp.zeros((half, PAIR), F32) for _ in range(2)]
        query_acc = [jnp.zeros((half, PAIR), F32) for _ in range(2)]
        for which in range(2):
            qm, km, vm, om = (half_mask(t, which) for t in (query, keys, values, mixed))
            for block in range(2):
                at = slice(block * half, (block + 1) * half)
                reach = (block + 1) * half
                s = dot_t(km[:reach], query[at]) + mask_s[:reach, at]
                s = jnp.exp(s - jnp.max(s, axis=0, keepdims=True))
                p = s * (1.0 / jnp.sum(s, axis=0, keepdims=True))
                grown = dot_t(vm[:reach], mixed[at])
                offset = jnp.sum(p * grown, axis=0, keepdims=True)
                ds = (p * (grown - offset)).astype(BF16)
                p = p.astype(BF16)
                query_acc[block] = query_acc[block] + dot_rows(ds, km[:reach])
                for piece in range(block + 1):
                    rs = slice(piece * half, (piece + 1) * half)
                    key_acc[piece] = key_acc[piece] + dot(ds[rs], qm[at])
                    value_acc[piece] = value_acc[piece] + dot(p[rs], om[at])
        for block in range(2):
            at = slice(block * half, (block + 1) * half)
            u = query_acc[block] * 0.125
            ql_s[at, to] = (u * cosine[at] - partner_of(u) * sine[at]).astype(BF16)
            u = key_acc[block]
            kl_s[at, to] = (u * cosine[at] - partner_of(u) * sine[at]).astype(BF16)
            vl_s[at, to] = value_acc[block].astype(BF16)
    a_all = a[...]
    qk_out[0] = dot_rows(a_all, ql_s[...]).astype(BF16)
    qk_out[1] = dot_rows(a_all, kl_s[...]).astype(BF16)
    vo_out[0] = dot_rows(a_all, vl_s[...]).astype(BF16)
    return dot_t(ql_s[...], wq[...]) + dot_t(kl_s[...], wk[...]) + dot_t(vl_s[...], wv[...])


def first_heads_back(ends, z_grad, a, cos, sin, q, k, v, o, wo, wq, wk, wv, qk_out, vo_out, a_grad, *scratch):
    a_grad[...] = heads_back(ends, z_grad, a, cos, sin, q, k, v, o, (wo, wq, wk, wv), qk_out, vo_out, *scratch)


def second_heads_back(core, ends, z_grad, a, cos, sin, q, k, v, o, a_first, own, other, h_grad, gain, wo, wq, wk, wv,
                      qk_out, vo_out, x_grad, gain_out, bias_out, x_s, *scratch):
    a_grad = a_first[...] + heads_back(
        ends, z_grad, a, cos, sin, q, k, v, o, (wo, wq, wk, wv), qk_out, vo_out, *scratch)
    write_rows(core, own, other, x_s)
    unit, scale = norm_parts(x_s[...].astype(F32))
    below, gains, biases = norm_back(a_grad, unit, scale, gain[...])
    x_grad[...] = (h_grad[...] + below).astype(BF16)
    gain_out[...] = gains
    bias_out[...] = biases


SMEM = pl.BlockSpec(memory_space=pltpu.SMEM)
FULL = pl.BlockSpec(memory_space=pltpu.VMEM)
FAR = pl.BlockSpec(memory_space=pltpu.HBM)


def params(limit, **kw):
    return pltpu.CompilerParams(vmem_limit_bytes=limit * 2**20, **kw)


def shape(dims, kind=BF16):
    return jax.ShapeDtypeStruct(dims, kind)


def call(kernel, operands, outs, scratch, smem, limit, far=0):
    specs = [SMEM] * smem + [FULL] * (len(operands) - smem - far) + [FAR] * far
    return pl.pallas_call(
        kernel,
        in_specs=specs,
        out_specs=[FULL] * len(outs),
        out_shape=outs,
        scratch_shapes=scratch,
        compiler_params=params(limit),
        cost_estimate=pl.CostEstimate(flops=COST, bytes_accessed=2**20, transcendentals=0),
    )(*operands)


def tiled(kernel, operands, kinds, outs, out_kinds, scratch, tile, steps, limit, first=0):
    def spec(kind, dims, first=0):
        if kind == "s":
            return SMEM
        if kind == "f":
            return pl.BlockSpec(dims, lambda i: (0,) * len(dims))
        if kind == "3":
            return pl.BlockSpec((1, *dims[1:]), lambda i: (i, 0, 0))
        if kind == "c":
            return pl.BlockSpec((dims[0], tile), lambda i: (0, i + first))
        return pl.BlockSpec((tile, dims[1]), lambda i: (i + first, 0))
    return pl.pallas_call(
        kernel,
        grid=(steps,),
        in_specs=[spec(kind, op.shape, first) for kind, op in zip(kinds, operands)],
        out_specs=[spec(kind, out.shape) for kind, out in zip(out_kinds, outs)],
        out_shape=outs,
        scratch_shapes=scratch,
        compiler_params=params(limit, dimension_semantics=("arbitrary",)),
        cost_estimate=pl.CostEstimate(flops=COST, bytes_accessed=2**20, transcendentals=0),
    )(*operands)


def swap(value):
    return lax.ppermute(value, "tensor", SWAP)


def coordinates(mesh):
    total = mesh.shape["dp"]
    places = [getattr(d, "coords", None) for d in mesh.devices.reshape(total, -1)[:, 0]]
    if all(p is not None and len(p) == 3 for p in places):
        sizes = [len({p[i] for p in places}) for i in range(3)]
        low = [min(p[i] for p in places) for i in range(3)]
        order = [((p[2] - low[2]) * sizes[1] + p[1] - low[1]) * sizes[0] + p[0] - low[0] for p in places]
        if order == list(range(total)):
            return tuple(sizes)
    return (2, 2, total // 4) if total % 4 == 0 else (1, 1, total)


def add(*terms):
    total = terms[0].astype(F32)
    for term in terms[1:]:
        total = total + term.astype(F32)
    return total.astype(BF16)


class Line:
    def __init__(self, token):
        self.token = token

    def fence(self, values):
        self.token, values = lax.optimization_barrier((self.token, values))
        return values

    def done(self, value):
        self.token = value
        return value


def settle_kernel(count, spots, *refs):
    *pieces, out = refs
    pieces = pieces[-4:]
    step = pl.program_id(0)
    size = pieces[0].shape[0]
    per = 4 // count
    for i, piece in enumerate(pieces):
        if count == 1:
            out[pl.ds(pl.multiple_of(spots[i] * size, size), size), :] = piece[...].astype(F32)
        else:
            @pl.when(spots[i] // per == step)
            def _():
                at = spots[i] % per
                out[pl.ds(pl.multiple_of(at * size, size), size), :] = piece[...].astype(F32)


def settle(spots, pieces, whole, dims, blocks, count):
    lines, columns = 4 * pieces[0].shape[0] // count, pieces[0].shape[1]
    before = [] if whole is None else [whole]
    base, last = blocks[0], blocks[-1]
    return pl.pallas_call(
        functools.partial(settle_kernel, count),
        grid=(count,),
        in_specs=[SMEM] + [pl.BlockSpec(memory_space=pl.ANY)] * len(before)
        + [pl.BlockSpec(p.shape, lambda i: (0, 0)) for p in pieces],
        out_specs=pl.BlockSpec((lines, columns), lambda i: (base[0], base[1] + i)),
        out_shape=shape(dims, F32),
        input_output_aliases={1: 0} if before else {},
        compiler_params=pltpu.CompilerParams(vmem_limit_bytes=20 * 2**20),
        cost_estimate=pl.CostEstimate(flops=COST, bytes_accessed=2**20, transcendentals=0),
    )(spots, *before, *pieces)


def settle_heads_kernel(folded, spots, *refs):
    pieces, (top, bottom) = refs[:4], refs[4:]
    size = pieces[0].shape[0]
    for i, piece in enumerate(pieces):
        for spot in range(4):
            @pl.when(spots[i] == spot)
            def _():
                at = spot % 2
                if spot < 2:
                    top[at * size:(at + 1) * size, :] = piece[...].astype(F32)
                elif folded:
                    bottom[:, at * size:(at + 1) * size] = piece[...].astype(F32)
                else:
                    bottom[at * size:(at + 1) * size, :] = piece[...].astype(F32)


def settle_heads(spots, pieces, folded):
    lines, columns = pieces[0].shape
    return pl.pallas_call(
        functools.partial(settle_heads_kernel, folded),
        in_specs=[SMEM] + [FULL] * 4,
        out_specs=[FULL, FULL],
        out_shape=[shape((2 * lines, columns), F32), shape((lines, 2 * columns) if folded else (2 * lines, columns), F32)],
        compiler_params=pltpu.CompilerParams(vmem_limit_bytes=12 * 2**20),
        cost_estimate=pl.CostEstimate(flops=COST, bytes_accessed=2**20, transcendentals=0),
    )(spots, *pieces)


class Chunk:
    def __init__(self, line, here, core, peer, finish):
        self.line, self.finish = line, finish
        self.own, self.other = None, swap(peer)
        self.a, self.z, self.b = jnp.where(core == 0, here[1], here[2]), here[4], jnp.where(core == 0, here[2], here[1])

    def part(self, value, *picks):
        value = value.reshape(*([2] * len(picks)), -1, value.shape[-1])
        for p in picks:
            value = lax.dynamic_index_in_dim(value, p, 0, keepdims=False)
        return value

    def trade(self, value, *bits):
        pairs = [(2 * i + c, 2 * (i ^ bits[c]) + c) for i in range(lax.axis_size("dp")) for c in range(2)]
        return lax.ppermute(value, ("dp", "tensor"), pairs)

    LANDS = {"c": "other", "a": "first", "b": "second", "d": "third", "e": "fourth", "f": "fifth",
             "g": "sixth", "h": "near", "k": "far"}

    def step(self, what):
        if what in self.LANDS:
            self.land(self.LANDS[what])
        else:
            getattr(self, "step" + what)()

    def land(self, name):
        setattr(self, name, self.line.fence(getattr(self, name)))

    def step0(self):
        own, other = self.line.fence((self.own, self.other))
        send = self.line.done(add(self.part(own, 1 - self.a), self.part(other, 1 - self.a)))
        self.first = self.trade(send, 1, 2)

    def step1(self):
        own, other, first = self.line.fence((self.own, self.other, self.first))
        a, z = self.a, 1 - self.z
        send = self.line.done(add(self.part(own, a, z), self.part(other, a, z), self.part(first, z)))
        self.second = self.trade(send, 4, 4)

    def step2(self):
        own, other, first, second = self.line.fence((self.own, self.other, self.first, self.second))
        a, z, b = self.a, self.z, 1 - self.b
        send = self.line.done(add(self.part(own, a, z, b), self.part(other, a, z, b), self.part(first, z, b), self.part(second, b)))
        self.third = self.trade(send, 2, 1)

    def step3(self):
        own, other, first, second, third = self.line.fence((self.own, self.other, self.first, self.second, self.third))
        a, z, b = self.a, self.z, self.b
        self.kept = self.line.done(add(self.part(own, a, z, b), self.part(other, a, z, b), self.part(first, z, b),
                                       self.part(second, b), third))
        self.fourth = self.trade(self.kept, 8, 8)

    def step4(self):
        kept, fourth = self.line.fence((self.kept, self.fourth))
        self.total = self.line.done(add(kept, fourth))
        self.fifth = self.trade(self.total, 2, 1)

    def step5(self):
        total, fifth = self.line.fence((self.total, self.fifth))
        low = self.b == 0
        self.mine = self.line.done(jnp.concatenate([jnp.where(low, total, fifth), jnp.where(low, fifth, total)], axis=0))
        self.sixth = self.trade(self.mine, 4, 4)
        self.near = self.trade(self.mine, 1, 2)

    def step6(self):
        self.sixth = self.line.done(self.line.fence(self.sixth))
        self.far = self.trade(self.sixth, 1, 2)

    def step7(self):
        pieces = self.line.fence((self.mine, self.sixth, self.near, self.far))
        a, z = self.a, self.z
        spots = jnp.stack([2 * a + z, 2 * a + 1 - z, 2 * (1 - a) + z, 2 * (1 - a) + 1 - z])
        self.line.done(self.finish(spots, pieces))


class Norms(Chunk):
    def __init__(self, line, values):
        self.line, self.values = line, values
        self.bits = (None, 1, 2, 4, 8)

    def step(self, what):
        if not what.isdigit():
            return self.land("other")
        number = int(what)
        if number == 0:
            self.values = self.line.fence(self.values)
        else:
            values, other = self.line.fence((self.values, self.other))
            self.values = self.line.done(values + other)
        if number < len(self.bits):
            bit = self.bits[number]
            self.other = swap(self.values) if bit is None else self.trade(self.values, bit, bit)


class Spread(Chunk):
    def __init__(self, line, core, full):
        self.line, self.core = line, core
        self.parts = full.reshape(2, full.shape[0] // 2, full.shape[1])

    def step(self, what):
        if what == "0":
            parts = self.line.fence(self.parts)
            self.mine = lax.dynamic_index_in_dim(parts, self.core, 0, keepdims=False)
            self.other = swap(self.line.done(lax.dynamic_index_in_dim(parts, 1 - self.core, 0, keepdims=False)))
        elif what == "1":
            mine, other = self.line.fence((self.mine, self.other))
            first = self.core == 0
            self.result = self.line.done(jnp.stack([jnp.where(first, mine, other), jnp.where(first, other, mine)]))
        else:
            self.land("other")


ORDER = (
    "G00", "G01", "y00", "G10", "G11", "o0c", "y0c", "y01", "o00", "o1c", "o10", "K00", "K01", "K10", "o0a", "i0c",
    "i00", "o01", "i1c", "K11", "o1a", "i10", "o11", "i0a", "i01", "o0b", "o02", "i1a", "H0", "o1b", "i0b", "o0d",
    "i02", "i11", "h0c", "o12", "i0d", "i03", "h1c", "o03", "o1d", "o13", "H1", "i1b", "i0e", "i04", "h00", "o0e",
    "h10", "o1e", "i0f", "i05", "i12", "h0a", "x00", "x0c", "h01", "i0g", "i06", "x01", "h1a", "o14", "i0h", "h11",
    "i1d", "i13", "h0b", "h02", "i0k", "i07", "o1f", "o15", "n00", "h0d", "h03", "h1b", "h12", "o1h", "n0a", "o04",
    "h1d", "h13", "i1e", "i14", "o0f", "n01", "o1g", "o16", "i1f", "n0b", "o05", "o1k", "h0e", "i15", "h1e", "h04",
    "o0h", "h14", "o17", "o0g", "i1h", "n02", "o06", "h0f", "h1f", "h05", "n0d", "i1g", "h15", "o0k", "i16", "h0h",
    "n03", "o07", "h0g", "h06", "h1h", "i1k", "i17", "h1g", "h16", "n0e", "h0k", "h07", "n04", "n0f", "n05", "h1k",
    "h17",
)
LIMITS = {"a1": 10, "a2": 13, "u1": 15, "u2": 20, "g": 9, "k": 12, "l": 15, "h1": 19, "h2": 19}


def on_device(
    sizes, inputs, lengths, query_weight, key_weight, value_weight, output_weight, inner_weight, outer_weight,
    entry_gain, entry_bias, merge_gain, merge_bias, inlet_gain, inlet_bias, outlet_gain, outlet_bias, cotangent,
):
    core = lax.axis_index("tensor").astype(jnp.int32)
    core_s = core.reshape(1)
    half = inputs.shape[1]
    rows = 2 * half
    width = query_weight.shape[1]
    units = inner_weight.shape[1]
    feats = inputs.shape[2]
    row = lambda v: v.reshape(1, feats)
    pick = lambda v, i: lax.dynamic_index_in_dim(v, i, 0, keepdims=False)
    x_own = pick(inputs, core)
    x_other = swap(pick(inputs, 1 - core))
    wq2, wk2, wv2 = swap(query_weight), swap(key_weight), swap(value_weight)
    wo2, wi2, wf2 = swap(output_weight), swap(inner_weight), swap(outer_weight)
    y_own = pick(cotangent, core)
    y_other = swap(pick(cotangent, 1 - core))

    lens = pick(lengths, core)[0]
    slot = jnp.arange(lens.shape[0], dtype=jnp.int32)
    ends = jnp.sum(jnp.where(slot[None, :] <= slot[:, None], lens[None, :], 0), axis=1)
    index = jnp.arange(rows, dtype=jnp.int32)
    begin = jnp.max(jnp.where(index[:, None] >= ends[None, :], ends[None, :], 0), axis=1)
    place = (index - begin).astype(F32)
    lane = jnp.arange(PAIR, dtype=jnp.int32)
    rate = jnp.exp((lane % (HEAD // 2)).astype(F32) * (-math.log(10000.0) / (HEAD // 2)))
    angle = place[:, None] * rate[None, :]
    cos = jnp.cos(angle)
    sin = jnp.sin(angle) * jnp.where(lane % HEAD < HEAD // 2, -1.0, 1.0)[None, :]

    act = shape((rows, width))
    mask = pltpu.VMEM((rows, rows), F32)
    xbuf = pltpu.VMEM((rows, feats), BF16)
    vmem = lambda dims, kind=BF16: pltpu.VMEM(dims, kind)
    dma = lambda *dims: pltpu.SemaphoreType.DMA(dims)
    head_bufs = [vmem((feats, width))] * 3
    a, q1, k1, v1, o1 = call(
        first_heads,
        [core_s, ends, x_own, x_other, row(entry_gain), row(entry_bias), cos, sin, query_weight, key_weight, value_weight],
        [shape((rows, feats)), act, act, act, act], [xbuf, mask], 2, LIMITS["a1"])
    q2, k2, v2, o2, z, h, c = call(
        second_heads,
        [core_s, ends, x_own, x_other, a, cos, sin, o1,
         row(merge_gain), row(merge_bias), row(inlet_gain), row(inlet_bias), wq2, wk2, wv2, output_weight, wo2],
        [act, act, act, act, shape((rows, feats), F32), shape((rows, feats), F32), shape((rows, feats))],
        [xbuf, mask], 2, LIMITS["a2"])
    tile = 512
    steps = units // tile
    big = shape((rows, units))
    steep = shape((steps, rows, tile))
    unit_bufs = lambda n: [vmem((n, feats, tile)), vmem((n, tile, feats)), dma(n, 2)]
    e1, s1, n1 = call(first_units, [c, inner_weight, outer_weight],
                      [big, steep, shape((rows, feats), F32)], unit_bufs(steps), 0, LIMITS["u1"], 2)
    e2, s2, y, n_grad, outlet_gains, outlet_biases = call(
        second_units, [core_s, c, n1, h, y_own, y_other, row(outlet_gain), row(outlet_bias), wi2, wf2],
        [big, steep, shape((rows, feats)), shape((rows, feats)), shape((1, feats), F32), shape((1, feats), F32)],
        [xbuf, *unit_bufs(steps)], 1, LIMITS["u2"], 2)
    total = shape((rows, feats), F32)
    line = Line(n_grad)
    made = {"c": None}
    wholes = {}
    scratch = [mask] + [vmem((rows, width))] * 4
    grads = [shape((2, feats, width)), shape((2, feats, width))]

    def outer_step(pair, mine):
        e_in, n_in = line.fence(((e2, e1)[mine], n_grad))
        (out,) = tiled(outer_terms, [e_in, n_in], "cf", [shape((2 * tile, feats))], "r", [], 2 * tile, 1, LIMITS["g"], pair)
        line.done(out)
        return [out]

    def inner_step(pair, mine):
        ng, cc, slope, wi, wo = line.fence([n_grad, c, *((s2, wi2, wf2), (s1, inner_weight, outer_weight))[mine]])
        outs = [shape((2, feats, tile)), total]
        bufs = unit_bufs(2)
        with_first = lambda kernel: functools.partial(kernel, 2 * pair)
        if made["c"] is None:
            out, made["c"] = call(with_first(first_units_back), [ng, cc, slope, wi, wo], outs, bufs, 0, LIMITS["k"], 2)
        elif pair == steps // 2 - 1 and mine:
            out, made["h"], made["z"], made["sums"] = call(
                with_first(last_units_back),
                [core_s, ng, cc, slope, made["c"], y_own, y_other, h, z, row(inlet_gain), row(merge_gain), wi, wo],
                [outs[0], total, shape((rows, feats)), shape((4, feats), F32)], [xbuf, *bufs], 1, LIMITS["l"], 2)
        else:
            out, made["c"] = call(with_first(more_units_back), [ng, cc, slope, made["c"], wi, wo], outs, bufs, 0, LIMITS["k"], 2)
        line.done(out)
        return [out.reshape(2 * feats, tile)]

    def heads_step(mine):
        z_grad = line.fence(made["z"])
        if not mine:
            qk, vo, made["a"] = call(
                first_heads_back, [ends, z_grad, a, cos, sin, q2, k2, v2, o2, wo2, wq2, wk2, wv2],
                grads + [total], scratch, 1, LIMITS["h1"])
        else:
            qk, vo, made["x"], made["gain"], made["bias"] = call(
                second_heads_back,
                [core_s, ends, z_grad, a, cos, sin, q1, k1, v1, o1, made["a"], x_own, x_other, made["h"], row(entry_gain),
                 output_weight, query_weight, key_weight, value_weight],
                grads + [shape((rows, feats)), shape((1, feats), F32), shape((1, feats), F32)], [xbuf] + scratch, 2,
                LIMITS["h2"])
        line.done(qk)
        return [qk.reshape(2 * feats, width), vo.reshape(2 * feats, width)]

    place_of = lax.axis_index("dp").astype(jnp.int32)
    here = {bit: (place_of // bit) % 2 for bit in (1, 2, 4, 8)}
    outs = {"o": (units, feats), "i": (feats, units)}

    def finisher(name):
        kind, number = name[0], int(name[1])

        def finish(spots, pieces):
            if kind == "o":
                wholes["o"] = settle(spots, pieces, wholes.get("o"), outs["o"], [(number, 0)], 1)
                return wholes["o"]
            if kind == "i":
                wholes["i"] = settle(spots, pieces, wholes.get("i"), outs["i"], [(0, 2 * number), (0, 2 * number + 1)], 2)
                return wholes["i"]
            wholes[name] = settle_heads(spots, pieces, number == 1)
            return wholes[name][1]
        return finish

    chunks = {"y0": Spread(line, core, y)}
    fast = tuple(sizes) == (2, 2, 4)
    plain = {}

    def peers(name, peer):
        if fast:
            chunks[name] = Chunk(line, here, core, peer, finisher(name))
        else:
            plain[name] = peer

    def owns(name, own):
        if fast:
            chunks[name].own = own
        else:
            wholes[name] = lax.psum(add(own, swap(plain[name])), "dp").astype(F32)

    for what in ORDER:
        name, last = what[:-1], what[-1]
        if name[0] in "GK":
            which, mine = int(name[1]), int(last)
            (made_now,) = (outer_step if name[0] == "G" else inner_step)(which, mine)
            (peers, owns)[mine](("o" if name[0] == "G" else "i") + str(which), made_now)
        elif name == "H":
            mine = int(last)
            for i, made_now in enumerate(heads_step(mine)):
                (peers, owns)[mine]("h" + str(i), made_now)
            if mine:
                sums = made["sums"]
                norms = [made["gain"], made["bias"], sums[0:1], sums[1:2], sums[2:3], sums[3:4], outlet_gains, outlet_biases]
                chunks["n0"] = Norms(line, jnp.concatenate(norms, axis=0))
                chunks["x0"] = Spread(line, core, made["x"])
        elif fast or name in ("x0", "y0"):
            chunks[name].step(last)
    outputs, input_grad = chunks["y0"].result, chunks["x0"].result
    norms = chunks["n0"].values
    if not fast:
        norms = lax.psum(norms, ("dp", "tensor"))
    if not fast:
        wholes["o"] = jnp.concatenate([wholes["o" + str(i)] for i in range(steps // 2)], axis=0)
        wholes["i"] = jnp.concatenate(
            [half for i in range(steps // 2) for half in jnp.split(wholes["i" + str(i)], 2, axis=0)], axis=1)
        wholes["h0"] = jnp.split(wholes["h0"], 2, axis=0)
        value, folded = jnp.split(wholes["h1"], 2, axis=0)
        wholes["h1"] = [value, jnp.concatenate([folded[:width], folded[width:]], axis=1)]
    query_grad, key_grad = wholes["h0"]
    value_grad, output_grad = wholes["h1"]
    inner_grad, outer_grad = wholes["i"], wholes["o"]
    weight_grads = [query_grad, key_grad, value_grad, output_grad, inner_grad, outer_grad]
    return (outputs, input_grad, *weight_grads, *[norms[i] for i in range(8)])


def solution(mesh):
    rows = P(None, ("dp", "tensor"), None)
    columns, lines = P(None, "tensor"), P("tensor", None)
    weights = (columns, columns, columns, lines, columns, lines)
    return jax.shard_map(
        functools.partial(on_device, coordinates(mesh)),
        mesh=mesh,
        in_specs=(rows, P(None, "dp", None), *weights, *([P()] * 8), rows),
        out_specs=(rows, rows, *weights, *([P()] * 8)),
        check_vma=False,
    )
```
